256 devices in a mesh: freq: 16 (over z, y_lo), orb: 16 (over x, y_hi, core).
Axes of the slice: x: 4, y: 4 (y_hi: 2, y_lo: 2; y = y_hi * 2 + y_lo), z: 8, core: 2. Of those that a mesh axis runs over, the one named last changes fastest.
Arguments:
- green: float32 [16, 2, 1024, 1024], P('freq', None, 'orb'), may hold values from -0.1875 to 0.1875
- green_bar: float32 [16, 2, 1024, 1024], P('freq', None, 'orb'), may hold values from -1.5 to 1.5
Outputs:
- h_bar: float32 [2, 1024, 1024], P(None, 'orb', 'freq')
The draws below stay inside these ranges and needn't reach their ends.
All inputs are finite; a program needn't handle non-finite values.
Results may differ from the reference program's by a relative error of at most 0.0001.
Values sent between devices are 32-bit elements; how exact they have to be, the bound alone decides.
A program may use at most 64 MiB of HBM per device.

```python
import jax
import jax.numpy as jnp
from jax import lax

N = 1024
FREQS = 16


def level_of(stream_key, extent, shards, least, largest):
    def one(axis_at, blocks):
        steps = jax.random.uniform(jax.random.fold_in(jax.random.fold_in(stream_key, 6), axis_at), (blocks,), jnp.float32, least / len(shards), largest / len(shards))
        return jnp.repeat(jnp.exp(steps), extent[axis_at] // blocks).reshape((-1,) + (1,) * (len(extent) - axis_at - 1))

    loudness = one(*shards[0])
    for cut in shards[1:]:
        loudness = loudness * one(*cut)
    return loudness


def centred(rng, shape, deviation, limit, shards=(), held_as=jnp.bfloat16):
    loudness = level_of(rng, shape, shards, -0.22, 0.18) if shards else 1.0
    values = jax.random.normal(rng, shape, jnp.float32) * deviation * loudness
    return jnp.minimum(jnp.maximum(values, -limit), limit).astype(held_as)


def setup_inputs(seed: int = 0) -> dict:
    key_of = jax.random.split(jax.random.key(seed), 3)
    green = centred(key_of[0], (FREQS, 2, N, N), N ** -0.5, 0.1875, ((0, 16), (2, 16)), jnp.float32)
    green_bar = centred(key_of[1], (FREQS, 2, N, N), 0.25, 1.5, ((0, 16), (2, 16)), jnp.float32)
    return {"green": green, "green_bar": green_bar}


def complex_product(pattern, left_op, right_op):
    def real_dot(left_part, right_part):
        return jnp.einsum(pattern, left_part, right_part, precision=lax.Precision.HIGHEST, preferred_element_type=jnp.float32)

    real_part = real_dot(left_op[0], right_op[0]) - real_dot(left_op[1], right_op[1])
    imag_part = real_dot(left_op[0], right_op[1]) + real_dot(left_op[1], right_op[0])
    return jnp.stack([real_part, imag_part])


def reference(green, green_bar):
    def one_frequency(running_sum, inputs_now):
        green_now, bar_now = inputs_now
        transposed = jnp.transpose(green_now, (0, 2, 1))
        middle = complex_product("ik,kj->ij", bar_now, transposed)
        adjoint = complex_product("ik,kj->ij", transposed, middle)
        return running_sum + adjoint, None

    start_sum = jnp.zeros((2, N, N), jnp.float32)
    total_sum, unused = lax.scan(one_frequency, start_sum, (green, green_bar))
    return total_sum
```

```python
import jax
import jax.numpy as jnp
from jax import lax
from jax.experimental import pallas as pl
from jax.experimental.pallas import tpu as pltpu
from jax.sharding import PartitionSpec as P

ROWS = 64
N = 1024
GROUPS = 4
UNIT = 128
X, Z = 4, 8

XP, XM, XF, CB, CG, YB, CBF, YG, CGF, ZC, FIN = 0, 2, 4, 6, 7, 8, 10, 12, 16, 20, 48
COPIES = 56


def split(value):
    high = value.astype(jnp.bfloat16)
    return high, (value - high.astype(jnp.float32)).astype(jnp.bfloat16)


def matmul(left, right, transposed):
    dims = (((1,), (1 if transposed else 0,)), ((), ()))
    return lax.dot_general(left, right, dims, preferred_element_type=jnp.float32)


def three_pass(left_hi, left_lo, right_hi, right_lo, transposed):
    return (
        matmul(left_hi, right_hi, transposed)
        + matmul(left_hi, right_lo, transposed)
        + matmul(left_lo, right_hi, transposed)
    )


def device_at(x, h, z, low, core):
    return {"freq": z * 2 + low, "orb": x * 4 + h * 2 + core}


def kernel(
    g_ref, b_ref, out_ref,
    gc, ba, ga, l_hi, l_lo, w_hi, w_lo, a_hi, a_lo, part, zr, fs, fr,
    send, recv, fin,
):
    freq, orb = lax.axis_index("freq"), lax.axis_index("orb")
    z, low = freq // 2, freq % 2
    x, h, core = orb // 4, (orb // 2) % 2, orb % 2
    odd = z % 2

    x_next = device_at((x + 1) % X, h, z, low, core)
    x_prev = device_at((x + 3) % X, h, z, low, core)
    partner = device_at(x, 1 - h, z, low, core)
    other = device_at(x, h, z, low, 1 - core)
    z_next = device_at(x, h, (z + 1) % Z, low, core)
    z_prev = device_at(x, h, (z + 7) % Z, low, core)

    def owner(group, half):
        return device_at(group, odd, 2 * (z // 2) + h, core, half)

    def owner_is_me(group, half):
        return (x == group) & (h == odd) & (low == core) & (core == half)

    def copy(src, dst, number, target):
        return pltpu.make_async_remote_copy(
            src_ref=src, dst_ref=dst, send_sem=send.at[number], recv_sem=recv.at[number],
            device_id=target, device_id_type=pl.DeviceIdType.MESH,
        )

    barrier = pltpu.get_barrier_semaphore()

    def greet(target):
        pl.semaphore_signal(barrier, inc=1, device_id=target, device_id_type=pl.DeviceIdType.MESH)

    for target in (x_next, x_prev, partner, other, z_next, z_prev):
        greet(target)
    self_owner = (h == odd) & (low == core)
    for from_x in range(X):
        for from_low in range(2):
            itself = self_owner & (x == from_x) & (low == from_low)

            @pl.when(jnp.logical_not(itself))
            def _():
                greet(device_at(from_x, odd, 2 * (z // 2) + h, from_low, low))

    pl.semaphore_wait(barrier, 14 - self_owner.astype(jnp.int32))

    g, b = g_ref.at[0], b_ref.at[0]
    xp = [copy(g.at[p], gc.at[0, p], XP + p, x_next) for p in range(2)]
    xm = [copy(g.at[p], gc.at[1, p], XM + p, x_prev) for p in range(2)]
    xf = [copy(gc.at[0, 0], gc.at[2, 0], XF, x_next), copy(gc.at[1, 1], gc.at[2, 1], XF + 1, x_prev)]
    yb = [copy(b.at[p], ba.at[1, p], YB + p, partner) for p in range(2)]
    cb = copy(b, ba.at[0], CB, other)
    cg = copy(g, ga.at[0], CG, other)
    cbf = [copy(ba.at[1, p], ba.at[2, p], CBF + p, other) for p in range(2)]

    def lanes(group):
        return pl.ds(group * 256, 256)

    yg = [copy(g.at[:, :, lanes(i)], ga.at[1, :, :, lanes(i)], YG + i, partner) for i in range(GROUPS)]
    cgf = [copy(ga.at[1, :, :, lanes(i)], ga.at[2, :, :, lanes(i)], CGF + i, other) for i in range(GROUPS)]

    yb[0].start()
    xp[0].start()
    xm[1].start()
    cb.start()
    yb[1].start()
    xp[1].start()
    xm[0].start()
    cg.start()

    def fill_left(ref, from_x):
        high_r, low_r = split(ref[0])
        high_i, low_i = split(ref[1])
        top = pl.ds(pl.multiple_of(from_x * ROWS, ROWS), ROWS)
        bottom = pl.ds(pl.multiple_of(256 + from_x * ROWS, ROWS), ROWS)
        for dst, re, im in ((l_hi, high_r, high_i), (l_lo, low_r, low_i)):
            dst[top, :N] = re
            dst[top, N:] = -im
            dst[bottom, :N] = im
            dst[bottom, N:] = re

    def fill_bar(ref, slot):
        rows = pl.ds(slot * ROWS, ROWS)
        for p in range(2):
            w_hi[rows, pl.ds(p * N, N)], w_lo[rows, pl.ds(p * N, N)] = split(ref[p])

    def fill_rows(ref, slot, columns):
        for p in range(2):
            rows = pl.ds(p * 256 + slot * ROWS, ROWS)
            a_hi[rows, columns], a_lo[rows, columns] = split(ref[p, :, columns])

    fill_left(g, x)
    fill_bar(b, 0)
    fill_rows(g, 0, pl.ds(0, N))
    cb.wait_recv()
    fill_bar(ba.at[0], 1)
    cg.wait_recv()
    fill_rows(ga.at[0], 1, pl.ds(0, N))

    yb[0].wait_send()
    yg[0].start()
    xp[0].wait_recv()
    xf[0].start()
    xm[1].wait_recv()
    xf[1].start()
    yb[0].wait_recv()
    cbf[0].start()
    yb[1].wait_send()
    yg[1].start()
    yb[1].wait_recv()
    cbf[1].start()
    fill_bar(ba.at[1], 2)
    xp[1].wait_recv()
    fill_left(gc.at[0], (x + 3) % X)
    xm[0].wait_recv()
    fill_left(gc.at[1], (x + 1) % X)
    for c in cbf:
        c.wait_recv()
    fill_bar(ba.at[2], 3)
    yg[0].wait_recv()
    cgf[0].start()
    yg[0].wait_send()
    yg[2].start()
    for c in xf:
        c.wait_recv()
    fill_left(gc.at[2], (x + 2) % X)

    middle = three_pass(l_hi[...], l_lo[...], w_hi[...], w_lo[...], True)
    m_r, m_i = middle[:256], middle[256:]
    left = jnp.concatenate(
        [jnp.concatenate([m_r, -m_i], axis=1), jnp.concatenate([m_i, m_r], axis=1)], axis=0
    )
    left_hi, left_lo = split(left)
    l_hi[:, :512] = left_hi
    l_lo[:, :512] = left_lo

    def chain(group):
        sign = 1 if group % 2 == 0 else -1
        chains = []
        first = ZC + group * 7
        for direction, hops, base in ((sign, 4, 0), (-sign, 3, 4)):
            target = z_next if direction == 1 else z_prev
            steps = []
            for s in range(hops):
                dest = (z + direction * (hops - s) + Z) % Z
                src = part.at[group, dest] if s == 0 else zr.at[group, base + s - 1]
                steps.append((copy(src, zr.at[group, base + s], first + base + s, target), dest, base + s - 1))
            chains.append(steps)
        return chains

    chains = [chain(i) for i in range(GROUPS)]

    def advance(group, s):
        for steps in chains[group]:
            if s < len(steps):
                step, dest, before = steps[s]
                if s > 0:
                    steps[s - 1][0].wait_recv()
                    zr[group, before] += part[group, dest]
                step.start()

    def owner_copy(group, half):
        place = x * 2 + low
        src, dst = fs.at[group, pl.ds(half * ROWS, ROWS)], fr.at[place]
        remote = pltpu.make_async_remote_copy(
            src_ref=src, dst_ref=dst, send_sem=send.at[FIN + group * 2 + half], recv_sem=fin.at[place],
            device_id=owner(group, half), device_id_type=pl.DeviceIdType.MESH,
        )
        return remote, pltpu.make_async_copy(src, dst, fin.at[place])

    def finish(group):
        for steps in chains[group]:
            steps[-1][0].wait_recv()
        total = part[group, z] + zr[group, 3] + zr[group, 6]
        fs[group] = total.T
        for half in range(2):
            remote, local = owner_copy(group, half)
            itself = owner_is_me(group, half)

            @pl.when(itself)
            def _():
                local.start()

            @pl.when(jnp.logical_not(itself))
            def _():
                remote.start()

    for tick in range(GROUPS + 4):
        if tick < GROUPS:
            cols = lanes(tick)
            if tick > 0:
                yg[tick].wait_recv()
                cgf[tick].start()
            if tick == 0:
                yg[1].wait_send()
                yg[3].start()
            fill_rows(ga.at[1], 2, cols)
            cgf[tick].wait_recv()
            fill_rows(ga.at[2], 3, cols)
            total = three_pass(l_hi[:, :512], l_lo[:, :512], a_hi[:, cols], a_lo[:, cols], False)
            for to_x in range(X):
                for to_h in range(2):
                    columns = slice(to_h * UNIT, (to_h + 1) * UNIT)
                    part[tick, 2 * to_x + to_h, :ROWS] = total[to_x * ROWS:(to_x + 1) * ROWS, columns]
                    part[tick, 2 * to_x + to_h, ROWS:] = total[256 + to_x * ROWS:256 + (to_x + 1) * ROWS, columns]
            advance(tick, 0)
        for group in range(GROUPS):
            s = tick - group
            if 1 <= s <= 3:
                advance(group, s)
            elif s == 4:
                finish(group)

    for place in range(8):
        pltpu.make_async_remote_copy(
            src_ref=fs.at[0, pl.ds(0, ROWS)], dst_ref=fr.at[place], send_sem=send.at[FIN], recv_sem=fin.at[place],
            device_id=other, device_id_type=pl.DeviceIdType.MESH,
        ).wait_recv()
    total = fr[0]
    for place in range(1, 8):
        total = total + fr[place]
    out_ref[0] = total[:, :ROWS]
    out_ref[1] = total[:, ROWS:]

    for c in (*xp, *xm, *xf, cb, cg, yg[2], yg[3], *cbf, *cgf):
        c.wait_send()
    for group in range(GROUPS):
        for steps in chains[group]:
            for step, _, _ in steps:
                step.wait_send()
        for half in range(2):
            @pl.when(jnp.logical_not(owner_is_me(group, half)))
            def _():
                owner_copy(group, half)[0].wait_send()


def body(green, green_bar):
    f32, bf16 = jnp.float32, jnp.bfloat16
    vmem = pl.BlockSpec(memory_space=pltpu.VMEM)
    return pl.pallas_call(
        kernel,
        out_shape=jax.ShapeDtypeStruct((2, ROWS, ROWS), f32),
        in_specs=[vmem, vmem],
        out_specs=vmem,
        scratch_shapes=[
            pltpu.VMEM((3, 2, ROWS, N), f32),
            pltpu.VMEM((3, 2, ROWS, N), f32),
            pltpu.VMEM((3, 2, ROWS, N), f32),
            pltpu.VMEM((512, 2 * N), bf16),
            pltpu.VMEM((512, 2 * N), bf16),
            pltpu.VMEM((256, 2 * N), bf16),
            pltpu.VMEM((256, 2 * N), bf16),
            pltpu.VMEM((512, N), bf16),
            pltpu.VMEM((512, N), bf16),
            pltpu.VMEM((GROUPS, Z, UNIT, UNIT), f32),
            pltpu.VMEM((GROUPS, 7, UNIT, UNIT), f32),
            pltpu.VMEM((GROUPS, UNIT, UNIT), f32),
            pltpu.VMEM((8, ROWS, UNIT), f32),
            pltpu.SemaphoreType.DMA((COPIES,)),
            pltpu.SemaphoreType.DMA((COPIES,)),
            pltpu.SemaphoreType.DMA((8,)),
        ],
        compiler_params=pltpu.CompilerParams(
            collective_id=0, has_side_effects=True, vmem_limit_bytes=40 * 1024 * 1024
        ),
        cost_estimate=pl.CostEstimate(flops=3 * 1073741824, bytes_accessed=1081344, transcendentals=0),
        name="dyson_adjoint",
    )(green, green_bar)


def solution(mesh):
    spec = P("freq", None, "orb", None)
    return jax.shard_map(
        body, mesh=mesh, in_specs=(spec, spec), out_specs=P(None, "orb", "freq"), check_vma=False
    )
```

```python
import jax
import jax.numpy as jnp
from jax import lax
from jax.experimental import pallas as pl
from jax.experimental.pallas import tpu as pltpu
from jax.sharding import PartitionSpec as P

ROWS = 64
N = 1024
GROUPS = 4
WIDE = 256
LANES = 128
X, Z = 4, 8
HOPS = 7
COPIES = 120


def split(value):
    high = value.astype(jnp.bfloat16)
    return high, (value - high.astype(jnp.float32)).astype(jnp.bfloat16)


def matmul(left, right, transposed):
    dims = (((1,), (1 if transposed else 0,)), ((), ()))
    return lax.dot_general(left, right, dims, preferred_element_type=jnp.float32)


def three_pass(left_hi, left_lo, right_hi, right_lo, transposed):
    return (
        matmul(left_hi, right_hi, transposed)
        + matmul(left_hi, right_lo, transposed)
        + matmul(left_lo, right_hi, transposed)
    )


def device_at(x, h, z, low, core):
    return {"freq": z * 2 + low, "orb": x * 4 + h * 2 + core}


def kernel(
    g_hbm, b_hbm, out_ref,
    g, b, gc, ba, ga, l_hi, l_lo, w_hi, w_lo, m_hi, m_lo, a_hi, a_lo,
    part_z, part_x, got_z, got_x, sum_x, hop_x, own_z, own_x, end_z, end_x, turn,
    send, recv, fin_z, fin_x, load,
):
    freq, orb = lax.axis_index("freq"), lax.axis_index("orb")
    z, low = freq // 2, freq % 2
    x, h, core = orb // 4, (orb // 2) % 2, orb % 2
    odd, pair = z % 2, z // 2

    x_next = device_at((x + 1) % X, h, z, low, core)
    x_far = device_at((x + 2) % X, h, z, low, core)
    x_prev = device_at((x + 3) % X, h, z, low, core)
    partner = device_at(x, 1 - h, z, low, core)
    other = device_at(x, h, z, low, 1 - core)
    z_next = device_at(x, h, (z + 1) % Z, low, core)
    z_prev = device_at(x, h, (z + 7) % Z, low, core)

    load_g = pltpu.make_async_copy(g_hbm.at[0], g, load.at[0])
    load_b = pltpu.make_async_copy(b_hbm.at[0], b, load.at[1])
    load_g.start()
    load_b.start()

    numbers = iter(range(COPIES))

    def copy(src, dst, target):
        number = next(numbers)
        return pltpu.make_async_remote_copy(
            src_ref=src, dst_ref=dst, send_sem=send.at[number], recv_sem=recv.at[number],
            device_id=target, device_id_type=pl.DeviceIdType.MESH,
        )

    barrier = pltpu.get_barrier_semaphore()

    def greet(target):
        pl.semaphore_signal(barrier, inc=1, device_id=target, device_id_type=pl.DeviceIdType.MESH)

    def greet_unless(itself, target):
        @pl.when(jnp.logical_not(itself))
        def _():
            greet(target)

    for target in (x_next, x_prev, x_far, partner, other, z_next, z_prev):
        greet(target)
    self_z = (h == odd) & (low == core)
    self_x = self_z & (x == pair)
    for from_x in range(X):
        for from_low in range(2):
            greet_unless(
                self_z & (x == from_x) & (low == from_low),
                device_at(from_x, odd, 2 * pair + h, from_low, low),
            )
    for from_pair in range(Z // 2):
        for from_low in range(2):
            greet_unless(
                self_x & (pair == from_pair) & (low == from_low),
                device_at(pair, odd, 2 * from_pair + h, from_low, low),
            )
    pl.semaphore_wait(barrier, 23 - self_z.astype(jnp.int32) - self_x.astype(jnp.int32))

    def wide(group):
        return pl.ds(group * WIDE, WIDE)

    gh, bh = g_hbm.at[0], b_hbm.at[0]
    yb = [copy(bh.at[p], ba.at[1, p], partner) for p in range(2)]
    xp = [copy(gh.at[p], gc.at[0, p], x_next) for p in range(2)]
    xm = [copy(gh.at[p], gc.at[1, p], x_prev) for p in range(2)]
    cb = copy(bh, ba.at[0], other)
    cg = copy(gh, ga.at[0], other)
    yg = [copy(gh.at[:, :, wide(i)], ga.at[1, :, :, wide(i)], partner) for i in range(GROUPS)]
    for c in (yb[0], xp[0], xm[1], cb, yb[1], xp[1], xm[0], cg, *yg):
        c.start()
    xf = [copy(gc.at[0, 0], gc.at[2, 0], x_next), copy(gc.at[1, 1], gc.at[2, 1], x_prev)]
    cbf = [copy(ba.at[1, p], ba.at[2, p], other) for p in range(2)]
    cgf = [copy(ga.at[1, :, :, wide(i)], ga.at[2, :, :, wide(i)], other) for i in range(GROUPS)]

    def fill_left(ref, place):
        high_r, low_r = split(ref[0])
        high_i, low_i = split(ref[1])
        for dst, re, im in ((l_hi, high_r, high_i), (l_lo, low_r, low_i)):
            for half in range(2):
                rows = slice(half * 32, half * 32 + 32)
                top = pl.ds(place * 128 + half * 64, 32)
                bottom = pl.ds(place * 128 + half * 64 + 32, 32)
                dst[top, :N] = re[rows]
                dst[top, N:] = -im[rows]
                dst[bottom, :N] = im[rows]
                dst[bottom, N:] = re[rows]

    def fill_bar(ref, slot):
        rows = pl.ds(slot * ROWS, ROWS)
        for p in range(2):
            w_hi[rows, pl.ds(p * N, N)], w_lo[rows, pl.ds(p * N, N)] = split(ref[p])

    def fill_rows(ref, slot, columns):
        for p in range(2):
            rows = pl.ds(p * 256 + slot * ROWS, ROWS)
            a_hi[rows, columns], a_lo[rows, columns] = split(ref[p, :, columns])

    def middle(start, count):
        rows = pl.ds(start * 128, count * 128)
        product = three_pass(l_hi[rows, :], l_lo[rows, :], w_hi[...], w_lo[...], True)
        for piece in range(start * 2, (start + count) * 2):
            at = (piece - start * 2) * 64
            re, im = product[at:at + 32], product[at + 32:at + 64]
            for first, second, rows in ((re, -im, pl.ds(piece * 64, 32)), (im, re, pl.ds(piece * 64 + 32, 32))):
                m_hi[rows, :256], m_lo[rows, :256] = split(first)
                m_hi[rows, 256:], m_lo[rows, 256:] = split(second)

    load_g.wait()
    fill_left(g, 0)
    fill_rows(g, 0, pl.ds(0, N))
    load_b.wait()
    fill_bar(b, 0)
    cb.wait_recv()
    fill_bar(ba.at[0], 1)
    cg.wait_recv()
    fill_rows(ga.at[0], 1, pl.ds(0, N))

    xp[0].wait_recv()
    xf[0].start()
    xm[1].wait_recv()
    xf[1].start()
    yb[0].wait_recv()
    cbf[0].start()
    xp[1].wait_recv()
    fill_left(gc.at[0], 2)
    xm[0].wait_recv()
    fill_left(gc.at[1], 1)
    yb[1].wait_recv()
    cbf[1].start()
    fill_bar(ba.at[1], 2)
    for c in cbf:
        c.wait_recv()
    fill_bar(ba.at[2], 3)
    middle(0, 3)
    yg[0].wait_recv()
    cgf[0].start()
    for c in xf:
        c.wait_recv()
    fill_left(gc.at[2], 3)
    middle(3, 1)

    def chains_of(group, own_part, got):
        sign = 1 if group % 2 == 0 else -1
        chains = []
        for direction, hops, base in ((sign, 4, 0), (-sign, 3, 4)):
            target = z_next if direction == 1 else z_prev
            steps = []
            for s in range(hops):
                dest = (z + direction * (hops - s) + Z) % Z
                before = got.at[group, base + s - 1]
                steps.append((copy(own_part(dest) if s == 0 else before, got.at[group, base + s], target), dest, before))
            chains.append(steps)
        return chains

    def unit_z(group):
        return lambda dest: part_z.at[group, ((dest // 2 - x + X) % X) * 2 + dest % 2]

    def unit_x(group):
        return lambda dest: hop_x.at[group, dest]

    chains_z = [chains_of(i, unit_z(i), got_z) for i in range(GROUPS)]
    chains_x = [chains_of(i, unit_x(i), got_x) for i in range(GROUPS)]
    to_x = [
        [copy(part_x.at[i, j], sum_x.at[i, j - 1], target) for j, target in ((1, x_next), (2, x_far), (3, x_prev))]
        for i in range(GROUPS)
    ]

    def advance(chains, own_part, s):
        for steps in chains:
            if s < len(steps):
                step, dest, before = steps[s]
                if s > 0:
                    steps[s - 1][0].wait_recv()
                    before[...] += own_part(dest)[...]
                step.start()

    def end_copy(src, dst, arrived, target, itself):
        number = next(numbers)
        remote = pltpu.make_async_remote_copy(
            src_ref=src, dst_ref=dst, send_sem=send.at[number], recv_sem=arrived,
            device_id=target, device_id_type=pl.DeviceIdType.MESH,
        )
        return remote, pltpu.make_async_copy(src, dst, arrived), itself

    place_z, place_x = x * 2 + low, pair * 2 + low
    ends_z = [[
        end_copy(
            own_z.at[i, half], end_z.at[place_z], fin_z.at[place_z],
            device_at(i, odd, 2 * pair + h, core, half), self_z & (x == i) & (core == half),
        ) for half in range(2)] for i in range(GROUPS)]
    ends_x = [[
        end_copy(
            own_x.at[i], end_x.at[place_x], fin_x.at[place_x],
            device_at(i, odd, 2 * x + h, core, half), self_x & (x == i) & (core == half),
        ) for half in range(2)] for i in range(GROUPS)]

    def start_ends(ends):
        for remote, local, itself in ends:
            @pl.when(itself)
            def _():
                local.start()

            @pl.when(jnp.logical_not(itself))
            def _():
                remote.start()

    def wait_ends(ends):
        for remote, local, itself in ends:
            @pl.when(jnp.logical_not(itself))
            def _():
                remote.wait_send()

    def forward(group):
        yg[group].wait_recv()
        cgf[group].start()

    def second(group):
        cols = wide(group)
        fill_rows(ga.at[1], 2, cols)
        cgf[group].wait_recv()
        fill_rows(ga.at[2], 3, cols)
        total = three_pass(m_hi[...], m_lo[...], a_hi[:, cols], a_lo[:, cols], False)
        for place, j in ((0, 0), (1, 1), (2, 3), (3, 2)):
            for side in range(2):
                lanes = slice(side * LANES, (side + 1) * LANES)
                part_z[group, j * 2 + side] = total[place * 128:place * 128 + 64, lanes]
                part_x[group, j, side] = total[place * 128 + 64:place * 128 + 128, lanes]
        for c in to_x[group]:
            c.start()
        advance(chains_z[group], unit_z(group), 0)

    def along_x(group):
        for c in to_x[group]:
            c.wait_recv()
        total = (part_x[group, 0] + sum_x[group, 0]) + (sum_x[group, 1] + sum_x[group, 2])
        for side in range(2):
            for q in range(4):
                hop_x[group, q * 2 + side] = total[side, q * 16:(q + 1) * 16]
        advance(chains_x[group], unit_x(group), 0)

    def finish_z(group):
        for steps in chains_z[group]:
            steps[-1][0].wait_recv()
        total = unit_z(group)(z)[...] + got_z[group, 3] + got_z[group, 6]
        flipped = total.T
        for half in range(2):
            top = flipped[half * 64:half * 64 + 32]
            bottom = flipped[half * 64 + 32:half * 64 + 64]
            own_z[group, half] = jnp.concatenate([top, bottom], axis=1)
        start_ends(ends_z[group])

    def finish_x(group):
        for steps in chains_x[group]:
            steps[-1][0].wait_recv()
        own_x[group] = hop_x[group, z] + got_x[group, 3] + got_x[group, 6]
        start_ends(ends_x[group])

    def clear_first():
        for c in (*xp, *xm, *xf, cb, cg, *yb, *cbf):
            c.wait_send()

    def clear(group):
        for c in (yg[group], cgf[group], *to_x[group]):
            c.wait_send()
        for steps in (*chains_z[group], *chains_x[group]):
            for step, _, _ in steps:
                step.wait_send()

    when = (20.5, 22.0, 24.5, 27.2)
    events = []
    for i in range(GROUPS):
        if i > 0:
            events.append((when[i] - 1.5, forward, (i,)))
        events.append((when[i], second, (i,)))
        for s in range(1, 4):
            events.append((when[i] + 2.2 * s, advance, (chains_z[i], unit_z(i), s)))
        events.append((when[i] + 8.8, finish_z, (i,)))
        events.append((when[i] + 3.9, along_x, (i,)))
        for s in range(1, 4):
            events.append((when[i] + 3.9 + 1.5 * s, advance, (chains_x[i], unit_x(i), s)))
        events.append((when[i] + 9.9, finish_x, (i,)))
        events.append((when[i] + 11.5, clear, (i,)))
    events.append((when[3] + 4.5, clear_first, ()))
    for _, action, arguments in sorted(events, key=lambda e: e[0]):
        action(*arguments)

    def arrived(refs, sems):
        for place in range(8):
            pltpu.make_async_copy(refs.at[place], refs.at[place], sems.at[place]).wait()

    arrived(end_z, fin_z)
    total = end_z[0]
    for place in range(1, 8):
        total = total + end_z[place]
    first = jnp.concatenate([total[:, :64], total[:, 64:]], axis=0)
    arrived(end_x, fin_x)
    pieces = [end_x[q * 2] + end_x[q * 2 + 1] for q in range(4)]
    turn[...] = jnp.concatenate(pieces, axis=0).T
    second_half = turn[pl.ds(pl.multiple_of(core * ROWS, ROWS), ROWS), :]
    for p in range(2):
        lanes = slice(p * 32, p * 32 + 32)
        out_ref[p] = jnp.concatenate([first[:, lanes], second_half[:, lanes]], axis=1)

    for i in range(GROUPS):
        wait_ends(ends_z[i])
        wait_ends(ends_x[i])


def body(green, green_bar):
    f32, bf16 = jnp.float32, jnp.bfloat16
    far = pl.BlockSpec(memory_space=pltpu.HBM)
    return pl.pallas_call(
        kernel,
        out_shape=jax.ShapeDtypeStruct((2, ROWS, ROWS), f32),
        in_specs=[far, far],
        out_specs=pl.BlockSpec(memory_space=pltpu.VMEM),
        scratch_shapes=[
            pltpu.VMEM((2, ROWS, N), f32),
            pltpu.VMEM((2, ROWS, N), f32),
            pltpu.VMEM((3, 2, ROWS, N), f32),
            pltpu.VMEM((3, 2, ROWS, N), f32),
            pltpu.VMEM((3, 2, ROWS, N), f32),
            pltpu.VMEM((512, 2 * N), bf16),
            pltpu.VMEM((512, 2 * N), bf16),
            pltpu.VMEM((256, 2 * N), bf16),
            pltpu.VMEM((256, 2 * N), bf16),
            pltpu.VMEM((512, 512), bf16),
            pltpu.VMEM((512, 512), bf16),
            pltpu.VMEM((512, N), bf16),
            pltpu.VMEM((512, N), bf16),
            pltpu.VMEM((GROUPS, Z, 64, LANES), f32),
            pltpu.VMEM((GROUPS, X, 2, 64, LANES), f32),
            pltpu.VMEM((GROUPS, HOPS, 64, LANES), f32),
            pltpu.VMEM((GROUPS, HOPS, 16, LANES), f32),
            pltpu.VMEM((GROUPS, 3, 2, 64, LANES), f32),
            pltpu.VMEM((GROUPS, Z, 16, LANES), f32),
            pltpu.VMEM((GROUPS, 2, 32, LANES), f32),
            pltpu.VMEM((GROUPS, 16, LANES), f32),
            pltpu.VMEM((8, 32, LANES), f32),
            pltpu.VMEM((8, 16, LANES), f32),
            pltpu.VMEM((LANES, 64), f32),
            pltpu.SemaphoreType.DMA((COPIES,)),
            pltpu.SemaphoreType.DMA((COPIES,)),
            pltpu.SemaphoreType.DMA((8,)),
            pltpu.SemaphoreType.DMA((8,)),
            pltpu.SemaphoreType.DMA((2,)),
        ],
        compiler_params=pltpu.CompilerParams(
            collective_id=0, has_side_effects=True, vmem_limit_bytes=48 * 1024 * 1024
        ),
        cost_estimate=pl.CostEstimate(flops=3 * 1073741824, bytes_accessed=1081344, transcendentals=0),
        name="dyson_adjoint",
    )(green, green_bar)


def solution(mesh):
    spec = P("freq", None, "orb", None)
    return jax.shard_map(
        body, mesh=mesh, in_specs=(spec, spec), out_specs=P(None, "orb", "freq"), check_vma=False
    )
```

```python
import jax
import jax.numpy as jnp
from jax import lax
from jax.experimental import pallas as pl
from jax.experimental.pallas import tpu as pltpu
from jax.sharding import PartitionSpec as P

ROWS = 64
N = 1024
QUARTERS = 4
GROUPS = ((0, 2), (2, 1), (3, 1))
WIDE = 256
LANES = 128
X, Z = 4, 8
HOPS = 7
COPIES = 112


def split(value):
    high = value.astype(jnp.bfloat16)
    return high, (value - high.astype(jnp.float32)).astype(jnp.bfloat16)


def matmul(left, right, transposed):
    dims = (((1,), (1 if transposed else 0,)), ((), ()))
    return lax.dot_general(left, right, dims, preferred_element_type=jnp.float32)


def three_pass(left_hi, left_lo, right_hi, right_lo, transposed):
    return (
        matmul(left_hi, right_hi, transposed)
        + matmul(left_hi, right_lo, transposed)
        + matmul(left_lo, right_hi, transposed)
    )


def device_at(x, h, z, low, core):
    return {"freq": z * 2 + low, "orb": x * 4 + h * 2 + core}


def kernel(
    g_hbm, b_hbm, out_ref,
    g, b, gc, ba, ga, l_hi, l_lo, w_hi, w_lo, m_hi, m_lo, a_hi, a_lo,
    part_z, part_x, got_z, got_x, sum_x, hop_x, own_z, own_x, end_z, end_x, turn,
    send, recv, fin_z, fin_x, load, nods,
):
    freq, orb = lax.axis_index("freq"), lax.axis_index("orb")
    z, low = freq // 2, freq % 2
    x, h, core = orb // 4, (orb // 2) % 2, orb % 2
    odd, pair = z % 2, z // 2

    x_next = device_at((x + 1) % X, h, z, low, core)
    x_far = device_at((x + 2) % X, h, z, low, core)
    x_prev = device_at((x + 3) % X, h, z, low, core)
    partner = device_at(x, 1 - h, z, low, core)
    other = device_at(x, h, z, low, 1 - core)
    z_next = device_at(x, h, (z + 1) % Z, low, core)
    z_prev = device_at(x, h, (z + 7) % Z, low, core)

    load_g = pltpu.make_async_copy(g_hbm.at[0], g, load.at[0])
    load_b = pltpu.make_async_copy(b_hbm.at[0], b, load.at[1])
    load_g.start()
    load_b.start()

    numbers = iter(range(COPIES))

    def copy(src, dst, target):
        number = next(numbers)
        return pltpu.make_async_remote_copy(
            src_ref=src, dst_ref=dst, send_sem=send.at[number], recv_sem=recv.at[number],
            device_id=target, device_id_type=pl.DeviceIdType.MESH,
        )

    barrier = pltpu.get_barrier_semaphore()

    def greet(target):
        pl.semaphore_signal(barrier, inc=1, device_id=target, device_id_type=pl.DeviceIdType.MESH)

    twin = device_at(x, h, z, 1 - low, core)
    for target in (x_next, x_prev, partner, other, z_next, z_prev, twin):
        greet(target)
    self_z = (h == odd) & (low == core)
    self_x = self_z & (x == pair)
    pl.semaphore_wait(barrier, 7)

    def nod(number, *targets):
        for target in targets:
            pl.semaphore_signal(
                nods.at[number], inc=1, device_id=target, device_id_type=pl.DeviceIdType.MESH
            )

    def wide(group):
        return pl.ds(group * WIDE, WIDE)

    gh, bh = g_hbm.at[0], b_hbm.at[0]
    yb = [copy(bh.at[p], ba.at[1, p], partner) for p in range(2)]
    xp = [copy(gh.at[p], gc.at[0, p], x_next) for p in range(2)]
    xm = [copy(gh.at[p], gc.at[1, p], x_prev) for p in range(2)]
    cb = copy(bh, ba.at[0], other)
    cg = copy(gh, ga.at[0], other)
    yg = [copy(gh.at[:, :, wide(i)], ga.at[1, :, :, wide(i)], partner) for i in range(QUARTERS)]
    for c in (yb[0], xp[0], xm[1], cb, yb[1], xp[1], xm[0], cg, *yg):
        c.start()
    xf = [copy(gc.at[0, 0], gc.at[2, 0], x_next), copy(gc.at[1, 1], gc.at[2, 1], x_prev)]
    cbf = [copy(ba.at[1, p], ba.at[2, p], other) for p in range(2)]
    cgf = [copy(ga.at[1, :, :, wide(i)], ga.at[2, :, :, wide(i)], other) for i in range(QUARTERS)]

    def fill_left(ref, place):
        high_r, low_r = split(ref[0])
        high_i, low_i = split(ref[1])
        for dst, re, im in ((l_hi, high_r, high_i), (l_lo, low_r, low_i)):
            for half in range(2):
                rows = slice(half * 32, half * 32 + 32)
                top = pl.ds(place * 128 + half * 64, 32)
                bottom = pl.ds(place * 128 + half * 64 + 32, 32)
                dst[top, :N] = re[rows]
                dst[top, N:] = -im[rows]
                dst[bottom, :N] = im[rows]
                dst[bottom, N:] = re[rows]

    def fill_bar(ref, slot):
        rows = pl.ds(slot * ROWS, ROWS)
        for p in range(2):
            w_hi[rows, pl.ds(p * N, N)], w_lo[rows, pl.ds(p * N, N)] = split(ref[p])

    def fill_rows(ref, slot, columns):
        for p in range(2):
            rows = pl.ds(p * 256 + slot * ROWS, ROWS)
            a_hi[rows, columns], a_lo[rows, columns] = split(ref[p, :, columns])

    def middle(start, count):
        rows = pl.ds(start * 128, count * 128)
        product = three_pass(l_hi[rows, :], l_lo[rows, :], w_hi[...], w_lo[...], True)
        for piece in range(start * 2, (start + count) * 2):
            at = (piece - start * 2) * 64
            re, im = product[at:at + 32], product[at + 32:at + 64]
            for first, second, rows in ((re, -im, pl.ds(piece * 64, 32)), (im, re, pl.ds(piece * 64 + 32, 32))):
                m_hi[rows, :256], m_lo[rows, :256] = split(first)
                m_hi[rows, 256:], m_lo[rows, 256:] = split(second)

    nod(0, z_next, z_prev)
    load_g.wait()
    fill_left(g, 0)
    fill_rows(g, 0, pl.ds(0, N))
    load_b.wait()
    fill_bar(b, 0)
    cb.wait_recv()
    fill_bar(ba.at[0], 1)
    cg.wait_recv()
    fill_rows(ga.at[0], 1, pl.ds(0, N))

    pl.semaphore_wait(nods.at[0], 2)
    nod(1, z_next, z_prev)
    xp[0].wait_recv()
    xf[0].start()
    xm[1].wait_recv()
    xf[1].start()
    yb[0].wait_recv()
    cbf[0].start()
    pl.semaphore_wait(nods.at[1], 2)
    nod(2, z_next, z_prev)
    xp[1].wait_recv()
    fill_left(gc.at[0], 2)
    xm[0].wait_recv()
    fill_left(gc.at[1], 1)
    pl.semaphore_wait(nods.at[2], 2)
    yb[1].wait_recv()
    cbf[1].start()
    fill_bar(ba.at[1], 2)
    for c in cbf:
        c.wait_recv()
    fill_bar(ba.at[2], 3)
    middle(0, 3)
    yg[0].wait_recv()
    cgf[0].start()
    for c in xf:
        c.wait_recv()
    fill_left(gc.at[2], 3)
    middle(3, 1)

    def quarters(group):
        return pl.ds(*GROUPS[group])

    def chains_of(group, own_part, got):
        sign = 1 if group % 2 == 0 else -1
        at = quarters(group)
        chains = []
        for direction, hops, base in ((sign, 4, 0), (-sign, 3, 4)):
            target = z_next if direction == 1 else z_prev
            steps = []
            for s in range(hops):
                dest = (z + direction * (hops - s) + Z) % Z
                before = got.at[base + s - 1, at]
                steps.append((copy(own_part(dest) if s == 0 else before, got.at[base + s, at], target), dest, before))
            chains.append(steps)
        return chains

    def unit_z(group):
        return lambda dest: part_z.at[((dest // 2 - x + X) % X) * 2 + dest % 2, quarters(group)]

    def unit_x(group):
        return lambda dest: hop_x.at[dest, quarters(group)]

    chains_z = [chains_of(i, unit_z(i), got_z) for i in range(len(GROUPS))]
    direct_x = [
        [
            copy(unit_x(i)((z + o) % Z), got_x.at[o - 1, quarters(i)], device_at(x, h, (z + o) % Z, low, core))
            for o in (4, 3, 5, 2, 6, 1, 7)
        ]
        for i in range(len(GROUPS))
    ]
    to_x = [
        [
            copy(part_x.at[j, quarters(i)], sum_x.at[j - 1, quarters(i)], target)
            for j, target in ((2, x_far), (1, x_next), (3, x_prev))
        ]
        for i in range(len(GROUPS))
    ]

    def advance(chains, own_part, s):
        for steps in chains:
            if s < len(steps):
                step, dest, before = steps[s]
                if s > 0:
                    steps[s - 1][0].wait_recv()
                    before[...] += own_part(dest)[...]
                step.start()

    def end_copy(src, dst, arrived, target, itself):
        number = next(numbers)
        remote = pltpu.make_async_remote_copy(
            src_ref=src, dst_ref=dst, send_sem=send.at[number], recv_sem=arrived,
            device_id=target, device_id_type=pl.DeviceIdType.MESH,
        )
        return remote, pltpu.make_async_copy(src, dst, arrived), itself

    place_z, place_x = x * 2 + low, pair * 2 + low
    ends_z = [[
        end_copy(
            own_z.at[i, half], end_z.at[place_z], fin_z.at[place_z],
            device_at(i, odd, 2 * pair + h, core, half), self_z & (x == i) & (core == half),
        ) for half in range(2)] for i in range(QUARTERS)]
    ends_x = [[
        end_copy(
            own_x.at[i], end_x.at[place_x], fin_x.at[place_x],
            device_at(i, odd, 2 * x + h, core, half), self_x & (x == i) & (core == half),
        ) for half in range(2)] for i in range(QUARTERS)]

    def start_ends(ends):
        for remote, local, itself in ends:
            @pl.when(itself)
            def _():
                local.start()

            @pl.when(jnp.logical_not(itself))
            def _():
                remote.start()

    def wait_ends(ends):
        for remote, local, itself in ends:
            @pl.when(jnp.logical_not(itself))
            def _():
                remote.wait_send()

    def forward(quarter):
        yg[quarter].wait_recv()
        cgf[quarter].start()

    def second(group):
        start, count = GROUPS[group]
        for quarter in range(start, start + count):
            cols = wide(quarter)
            fill_rows(ga.at[1], 2, cols)
            cgf[quarter].wait_recv()
            fill_rows(ga.at[2], 3, cols)
            total = three_pass(m_hi[...], m_lo[...], a_hi[:, cols], a_lo[:, cols], False)
            for place, j in ((0, 0), (1, 1), (2, 3), (3, 2)):
                for side in range(2):
                    lanes = slice(side * LANES, (side + 1) * LANES)
                    part_z[j * 2 + side, quarter] = total[place * 128:place * 128 + 64, lanes]
                    part_x[j, quarter, side] = total[place * 128 + 64:place * 128 + 128, lanes]
        for c in to_x[group]:
            c.start()
        advance(chains_z[group], unit_z(group), 0)

    def along_x(group):
        for c in to_x[group]:
            c.wait_recv()
        start, count = GROUPS[group]
        for i in range(start, start + count):
            total = (part_x[0, i] + sum_x[0, i]) + (sum_x[1, i] + sum_x[2, i])
            for side in range(2):
                for q in range(4):
                    hop_x[q * 2 + side, i] = total[side, q * 16:(q + 1) * 16]
        for c in direct_x[group]:
            c.start()

    def finish_z(group):
        for steps in chains_z[group]:
            steps[-1][0].wait_recv()
        start, count = GROUPS[group]
        sums = unit_z(group)(z)[...] + got_z[3, quarters(group)] + got_z[6, quarters(group)]
        for i in range(count):
            flipped = sums[i].T
            for half in range(2):
                top = flipped[half * 64:half * 64 + 32]
                bottom = flipped[half * 64 + 32:half * 64 + 64]
                own_z[start + i, half] = jnp.concatenate([top, bottom], axis=1)

    def finish_x(group):
        start, count = GROUPS[group]
        at = quarters(group)
        for c in direct_x[group]:
            c.wait_recv()
        sums = hop_x[z, at] + got_x[0, at]
        for o in range(1, 7):
            sums = sums + got_x[o, at]
        own_x[at] = sums

    def greet_twin():
        nod(3, twin)

    def hear_twin():
        pl.semaphore_wait(nods.at[3], 1)

    def hand_over(ends, group):
        start, count = GROUPS[group]
        for i in range(start, start + count):
            start_ends(ends[i])

    def clear_first():
        for c in (*xp, *xm, *xf, cb, cg, *yb, *cbf):
            c.wait_send()

    def clear(group):
        for c in to_x[group]:
            c.wait_send()
        start, count = GROUPS[group]
        for i in range(start, start + count):
            yg[i].wait_send()
            cgf[i].wait_send()
        for steps in chains_z[group]:
            for step, _, _ in steps:
                step.wait_send()
        for c in direct_x[group]:
            c.wait_send()

    for token in (
        "F1", "S0", "F2", "S1", "F3", "Z01", "S2", "Z11", "Z02", "Z21", "X0", "Z12", "Z03", "Z22", "X1",
        "C9", "X2", "Z13", "Z04", "D0", "T0", "Z23", "Z14", "T1", "P0", "Q0", "P1", "Z24", "P2", "C0", "D1",
        "Q1", "C1", "D2", "Q2", "C2",
    ):
        kind, at = token[0], int(token[1])
        if kind == "F":
            forward(at)
        elif kind == "S":
            second(at)
        elif kind == "X":
            along_x(at)
        elif kind == "D":
            finish_x(at)
        elif kind == "T":
            greet_twin() if at == 0 else hear_twin()
        elif kind == "P":
            hand_over(ends_z, at)
        elif kind == "Q":
            hand_over(ends_x, at)
        elif kind == "C":
            clear(at) if at < len(GROUPS) else clear_first()
        elif token[2] == "4":
            finish_z(at)
        else:
            advance(chains_z[at], unit_z(at), int(token[2]))

    def arrived(refs, sems):
        for place in range(8):
            pltpu.make_async_copy(refs.at[place], refs.at[place], sems.at[place]).wait()

    arrived(end_z, fin_z)
    total = end_z[0]
    for place in range(1, 8):
        total = total + end_z[place]
    first = jnp.concatenate([total[:, :64], total[:, 64:]], axis=0)
    arrived(end_x, fin_x)
    pieces = [end_x[q * 2] + end_x[q * 2 + 1] for q in range(4)]
    turn[...] = jnp.concatenate(pieces, axis=0).T
    second_half = turn[pl.ds(pl.multiple_of(core * ROWS, ROWS), ROWS), :]
    for p in range(2):
        lanes = slice(p * 32, p * 32 + 32)
        out_ref[p] = jnp.concatenate([first[:, lanes], second_half[:, lanes]], axis=1)

    for i in range(QUARTERS):
        wait_ends(ends_z[i])
        wait_ends(ends_x[i])


def body(green, green_bar):
    f32, bf16 = jnp.float32, jnp.bfloat16
    far = pl.BlockSpec(memory_space=pltpu.HBM)
    return pl.pallas_call(
        kernel,
        out_shape=jax.ShapeDtypeStruct((2, ROWS, ROWS), f32),
        in_specs=[far, far],
        out_specs=pl.BlockSpec(memory_space=pltpu.VMEM),
        scratch_shapes=[
            pltpu.VMEM((2, ROWS, N), f32),
            pltpu.VMEM((2, ROWS, N), f32),
            pltpu.VMEM((3, 2, ROWS, N), f32),
            pltpu.VMEM((3, 2, ROWS, N), f32),
            pltpu.VMEM((3, 2, ROWS, N), f32),
            pltpu.VMEM((512, 2 * N), bf16),
            pltpu.VMEM((512, 2 * N), bf16),
            pltpu.VMEM((256, 2 * N), bf16),
            pltpu.VMEM((256, 2 * N), bf16),
            pltpu.VMEM((512, 512), bf16),
            pltpu.VMEM((512, 512), bf16),
            pltpu.VMEM((512, N), bf16),
            pltpu.VMEM((512, N), bf16),
            pltpu.VMEM((Z, QUARTERS, 64, LANES), f32),
            pltpu.VMEM((X, QUARTERS, 2, 64, LANES), f32),
            pltpu.VMEM((HOPS, QUARTERS, 64, LANES), f32),
            pltpu.VMEM((HOPS, QUARTERS, 16, LANES), f32),
            pltpu.VMEM((3, QUARTERS, 2, 64, LANES), f32),
            pltpu.VMEM((Z, QUARTERS, 16, LANES), f32),
            pltpu.VMEM((QUARTERS, 2, 32, LANES), f32),
            pltpu.VMEM((QUARTERS, 16, LANES), f32),
            pltpu.VMEM((8, 32, LANES), f32),
            pltpu.VMEM((8, 16, LANES), f32),
            pltpu.VMEM((LANES, 64), f32),
            pltpu.SemaphoreType.DMA((COPIES,)),
            pltpu.SemaphoreType.DMA((COPIES,)),
            pltpu.SemaphoreType.DMA((8,)),
            pltpu.SemaphoreType.DMA((8,)),
            pltpu.SemaphoreType.DMA((2,)),
            pltpu.SemaphoreType.REGULAR((4,)),
        ],
        compiler_params=pltpu.CompilerParams(
            collective_id=0, has_side_effects=True, vmem_limit_bytes=63 * 1024 * 1024
        ),
        cost_estimate=pl.CostEstimate(flops=3 * 1073741824, bytes_accessed=1081344, transcendentals=0),
        name="dyson_adjoint",
    )(green, green_bar)


def solution(mesh):
    spec = P("freq", None, "orb", None)
    return jax.shard_map(
        body, mesh=mesh, in_specs=(spec, spec), out_specs=P(None, "orb", "freq"), check_vma=False
    )
```

```python
import jax
import jax.numpy as jnp
from jax import lax
from jax.experimental import pallas as pl
from jax.experimental.pallas import tpu as pltpu
from jax.sharding import PartitionSpec as P

ROWS = 64
N = 1024
QUARTERS = 4
GROUPS = ((0, 1), (1, 1), (2, 1), (3, 1))
WIDE = 256
LANES = 128
X, Z = 4, 8
HOPS = 7
COPIES = 160


def split(value):
    high = value.astype(jnp.bfloat16)
    return high, (value - high.astype(jnp.float32)).astype(jnp.bfloat16)


def matmul(left, right, transposed):
    dims = (((1,), (1 if transposed else 0,)), ((), ()))
    return lax.dot_general(left, right, dims, preferred_element_type=jnp.float32)


def three_pass(left_hi, left_lo, right_hi, right_lo, transposed):
    return (
        matmul(left_hi, right_hi, transposed)
        + matmul(left_hi, right_lo, transposed)
        + matmul(left_lo, right_hi, transposed)
    )


def device_at(x, h, z, low, core):
    return {"freq": z * 2 + low, "orb": x * 4 + h * 2 + core}


def kernel(
    g_hbm, b_hbm, out_ref,
    g, b, gc, ba, ga, l_hi, l_lo, w_hi, w_lo, m_hi, m_lo, a_hi, a_lo,
    part_z, part_x, got_z, got_x, sum_x, mid_x, sum_y, hop_x, own_z, own_x, end_z, end_x, turn,
    send, recv, fin_z, fin_x, load, nods,
):
    freq, orb = lax.axis_index("freq"), lax.axis_index("orb")
    z, low = freq // 2, freq % 2
    x, h, core = orb // 4, (orb // 2) % 2, orb % 2
    odd, pair = z % 2, z // 2

    x_next = device_at((x + 1) % X, h, z, low, core)
    x_far = device_at((x + 2) % X, h, z, low, core)
    x_prev = device_at((x + 3) % X, h, z, low, core)
    partner = device_at(x, 1 - h, z, low, core)
    other = device_at(x, h, z, low, 1 - core)
    z_next = device_at(x, h, (z + 1) % Z, low, core)
    z_prev = device_at(x, h, (z + 7) % Z, low, core)

    load_g = pltpu.make_async_copy(g_hbm.at[0], g, load.at[0])
    load_b = pltpu.make_async_copy(b_hbm.at[0], b, load.at[1])
    load_g.start()
    load_b.start()

    numbers = iter(range(COPIES))

    def copy(src, dst, target):
        number = next(numbers)
        return pltpu.make_async_remote_copy(
            src_ref=src, dst_ref=dst, send_sem=send.at[number], recv_sem=recv.at[number],
            device_id=target, device_id_type=pl.DeviceIdType.MESH,
        )

    barrier = pltpu.get_barrier_semaphore()

    def greet(target):
        pl.semaphore_signal(barrier, inc=1, device_id=target, device_id_type=pl.DeviceIdType.MESH)

    twin = device_at(x, h, z, 1 - low, core)
    for target in (x_next, x_prev, partner, other, z_next, z_prev, twin):
        greet(target)
    self_z = (h == odd) & (low == core)
    pl.semaphore_wait(barrier, 7)

    def nod(number, *targets):
        for target in targets:
            pl.semaphore_signal(
                nods.at[number], inc=1, device_id=target, device_id_type=pl.DeviceIdType.MESH
            )

    def wide(quarter):
        return pl.ds(quarter * WIDE, WIDE)

    def lanes_of(quarter, side):
        return pl.ds((quarter + 2 * side) % QUARTERS * WIDE + side * LANES, LANES)

    blocks = [[lanes_of(i, side) for side in range(2)] for i in range(QUARTERS)]

    gh, bh = g_hbm.at[0], b_hbm.at[0]
    yb = [copy(bh.at[p], ba.at[1, p], partner) for p in range(2)]
    xp = [copy(gh.at[p], gc.at[0, p], x_next) for p in range(2)]
    xm = [copy(gh.at[p], gc.at[1, p], x_prev) for p in range(2)]
    cb = copy(bh, ba.at[0], other)
    cg = copy(gh, ga.at[0], other)
    yg = [[copy(gh.at[:, :, k], ga.at[1, :, :, k], partner) for k in block] for block in blocks]
    for c in (yb[0], xp[0], xm[1], cb, yb[1], xp[1], xm[0], cg, *sum(yg, [])):
        c.start()
    xf = [copy(gc.at[0, 0], gc.at[2, 0], x_next), copy(gc.at[1, 1], gc.at[2, 1], x_prev)]
    cbf = [copy(ba.at[1, p], ba.at[2, p], other) for p in range(2)]
    cgf = [[copy(ga.at[1, :, :, k], ga.at[2, :, :, k], other) for k in block] for block in blocks]

    def fill_left(ref, place):
        high_r, low_r = split(ref[0])
        high_i, low_i = split(ref[1])
        for dst, re, im in ((l_hi, high_r, high_i), (l_lo, low_r, low_i)):
            for half in range(2):
                rows = slice(half * 32, half * 32 + 32)
                top = pl.ds(place * 128 + half * 64, 32)
                bottom = pl.ds(place * 128 + half * 64 + 32, 32)
                dst[top, :N] = re[rows]
                dst[top, N:] = -im[rows]
                dst[bottom, :N] = im[rows]
                dst[bottom, N:] = re[rows]

    def fill_bar(ref, slot):
        rows = pl.ds(slot * ROWS, ROWS)
        for p in range(2):
            w_hi[rows, pl.ds(p * N, N)], w_lo[rows, pl.ds(p * N, N)] = split(ref[p])

    def fill_rows(ref, slot, quarter):
        for p in range(2):
            rows = pl.ds(p * 256 + slot * ROWS, ROWS)
            for side in range(2):
                columns = pl.ds(quarter * WIDE + side * LANES, LANES)
                a_hi[rows, columns], a_lo[rows, columns] = split(ref[p, :, blocks[quarter][side]])

    def middle(start, count):
        rows = pl.ds(start * 128, count * 128)
        product = three_pass(l_hi[rows, :], l_lo[rows, :], w_hi[...], w_lo[...], True)
        for piece in range(start * 2, (start + count) * 2):
            at = (piece - start * 2) * 64
            re, im = product[at:at + 32], product[at + 32:at + 64]
            for first, second, rows in ((re, -im, pl.ds(piece * 64, 32)), (im, re, pl.ds(piece * 64 + 32, 32))):
                m_hi[rows, :256], m_lo[rows, :256] = split(first)
                m_hi[rows, 256:], m_lo[rows, 256:] = split(second)

    nod(0, z_next, z_prev)
    load_g.wait()
    fill_left(g, 0)
    for i in range(QUARTERS):
        fill_rows(g, 0, i)
    load_b.wait()
    fill_bar(b, 0)
    cb.wait_recv()
    fill_bar(ba.at[0], 1)
    cg.wait_recv()
    for i in range(QUARTERS):
        fill_rows(ga.at[0], 1, i)

    pl.semaphore_wait(nods.at[0], 2)
    nod(1, z_next, z_prev)
    nod(3, other)
    xp[0].wait_recv()
    xf[0].start()
    xm[1].wait_recv()
    xf[1].start()
    pl.semaphore_wait(nods.at[3], 1)
    nod(4, partner)
    yb[0].wait_recv()
    cbf[0].start()
    pl.semaphore_wait(nods.at[1], 2)
    nod(2, z_next, z_prev)
    pl.semaphore_wait(nods.at[4], 1)
    nod(5, twin)
    pl.semaphore_wait(nods.at[5], 1)
    nod(6, x_next, x_prev)
    xp[1].wait_recv()
    fill_left(gc.at[0], 2)
    xm[0].wait_recv()
    fill_left(gc.at[1], 1)
    pl.semaphore_wait(nods.at[2], 2)
    pl.semaphore_wait(nods.at[6], 2)
    nod(7, x_next, x_prev)
    yb[1].wait_recv()
    cbf[1].start()
    fill_bar(ba.at[1], 2)
    for c in cbf:
        c.wait_recv()
    fill_bar(ba.at[2], 3)
    pl.semaphore_wait(nods.at[7], 2)
    middle(0, 3)
    for side in range(2):
        yg[0][side].wait_recv()
        cgf[0][side].start()
    for c in xf:
        c.wait_recv()
    fill_left(gc.at[2], 3)
    middle(3, 1)

    def quarters(group):
        return pl.ds(*GROUPS[group])

    def chains_of(group, own_part, got):
        sign = 1 if group % 2 == 0 else -1
        at = quarters(group)
        chains = []
        for direction, hops, base in ((sign, 4, 0), (-sign, 3, 4)):
            target = z_next if direction == 1 else z_prev
            steps = []
            for s in range(hops):
                dest = (z + direction * (hops - s) + Z) % Z
                before = got.at[base + s - 1, at]
                steps.append((copy(own_part(dest) if s == 0 else before, got.at[base + s, at], target), dest, before))
            chains.append(steps)
        return chains

    def unit_z(group):
        return lambda dest: part_z.at[((dest // 2 - x + X) % X) * 2 + dest % 2, quarters(group)]

    def unit_x(group):
        return lambda dest: hop_x.at[dest, quarters(group)]

    chains_z = [chains_of(i, unit_z(i), got_z) for i in range(len(GROUPS))]
    direct_x = [
        [
            copy(unit_x(i)((z + o) % Z), got_x.at[o - 1, quarters(i)], device_at(x, h, (z + o) % Z, low, core))
            for o in (4, 3, 5, 2, 6, 1, 7)
        ]
        for i in range(len(GROUPS))
    ]
    to_twin = [copy(mid_x.at[1 - low, quarters(i)], sum_y.at[quarters(i)], twin) for i in range(len(GROUPS))]
    to_x = [
        [
            copy(part_x.at[(x + j) % X, quarters(i)], sum_x.at[j - 1, quarters(i)], target)
            for j, target in ((2, x_far), (1, x_next), (3, x_prev))
        ]
        for i in range(len(GROUPS))
    ]

    def advance(chains, own_part, s):
        for steps in chains:
            if s < len(steps):
                step, dest, before = steps[s]
                if s > 0:
                    steps[s - 1][0].wait_recv()
                    before[...] += own_part(dest)[...]
                step.start()

    def end_copy(src, dst, arrived, target, itself):
        number = next(numbers)
        remote = pltpu.make_async_remote_copy(
            src_ref=src, dst_ref=dst, send_sem=send.at[number], recv_sem=arrived,
            device_id=target, device_id_type=pl.DeviceIdType.MESH,
        )
        return remote, pltpu.make_async_copy(src, dst, arrived), itself

    place_z = place_x = x * 2 + low
    ends_z = [[
        end_copy(
            own_z.at[i, half], end_z.at[place_z], fin_z.at[place_z],
            device_at((i + 2 * odd) % X, odd, 2 * pair + h, core, half),
            self_z & (x == (i + 2 * odd) % X) & (core == half),
        ) for half in range(2)] for i in range(QUARTERS)]
    ends_x = [[
        end_copy(
            own_x.at[i], end_x.at[place_x], fin_x.at[place_x],
            device_at((i + 2 * odd) % X, odd, 2 * pair + h, core, half),
            self_z & (x == (i + 2 * odd) % X) & (core == half),
        ) for half in range(2)] for i in range(QUARTERS)]

    def start_ends(ends):
        for remote, local, itself in ends:
            @pl.when(itself)
            def _():
                local.start()

            @pl.when(jnp.logical_not(itself))
            def _():
                remote.start()

    def wait_ends(ends):
        for remote, local, itself in ends:
            @pl.when(jnp.logical_not(itself))
            def _():
                remote.wait_send()

    def forward(quarter):
        for side in range(2):
            yg[quarter][side].wait_recv()
            cgf[quarter][side].start()

    def second(group):
        start, count = GROUPS[group]
        for quarter in range(start, start + count):
            cols = wide(quarter)
            fill_rows(ga.at[1], 2, quarter)
            for c in cgf[quarter]:
                c.wait_recv()
            fill_rows(ga.at[2], 3, quarter)
            total = three_pass(m_hi[...], m_lo[...], a_hi[:, cols], a_lo[:, cols], False)
            for place, j in ((0, 0), (1, 1), (2, 3), (3, 2)):
                for side in range(2):
                    lanes = slice(side * LANES, (side + 1) * LANES)
                    part_z[j * 2 + side, quarter] = total[place * 128:place * 128 + 64, lanes]
                    for k in range(X):
                        rows = place * 128 + 64 + k * 16
                        part_x[k, quarter, 2 * ((x + j) % X) + side] = total[rows:rows + 16, lanes]
        for c in to_x[group]:
            c.start()
        advance(chains_z[group], unit_z(group), 0)

    def along_x(group):
        for c in to_x[group]:
            c.wait_recv()
        start, count = GROUPS[group]
        for i in range(start, start + count):
            total = (part_x[x, i] + sum_x[0, i]) + (sum_x[1, i] + sum_x[2, i])
            for part in range(2):
                mid_x[part, i] = total[:, part * 8:part * 8 + 8]
        to_twin[group].start()

    def along_y(group):
        to_twin[group].wait_recv()
        start, count = GROUPS[group]
        for i in range(start, start + count):
            hop_x[:, i] = mid_x[low, i] + sum_y[i]
        for c in direct_x[group]:
            c.start()

    def finish_z(group):
        for steps in chains_z[group]:
            steps[-1][0].wait_recv()
        start, count = GROUPS[group]
        sums = unit_z(group)(z)[...] + got_z[3, quarters(group)] + got_z[6, quarters(group)]
        for i in range(count):
            flipped = sums[i].T
            for half in range(2):
                top = flipped[half * 64:half * 64 + 32]
                bottom = flipped[half * 64 + 32:half * 64 + 64]
                own_z[start + i, half] = jnp.concatenate([top, bottom], axis=1)

    def finish_x(group):
        start, count = GROUPS[group]
        at = quarters(group)
        for c in direct_x[group]:
            c.wait_recv()
        sums = hop_x[z, at] + got_x[0, at]
        for o in range(1, 7):
            sums = sums + got_x[o, at]
        own_x[at] = sums

    def hand_over(ends, group):
        start, count = GROUPS[group]
        for i in range(start, start + count):
            start_ends(ends[i])

    def clear_first():
        for c in (*xp, *xm, *xf, cb, cg, *yb, *cbf):
            c.wait_send()

    def clear(group):
        for c in to_x[group]:
            c.wait_send()
        start, count = GROUPS[group]
        for i in range(start, start + count):
            for c in (*yg[i], *cgf[i]):
                c.wait_send()
        for steps in chains_z[group]:
            for step, _, _ in steps:
                step.wait_send()
        to_twin[group].wait_send()
        for c in direct_x[group]:
            c.wait_send()

    for token in (
        "F1", "S0", "F2", "S1", "F3", "Z01", "S2", "Z11", "X0", "S3", "Z02", "Z21", "X1", "Z12", "Y0", "Z31",
        "X2", "Z03", "C9", "Z22", "Y1", "X3", "Z13", "Z32", "Y2", "D0", "Q0", "Z04", "P0", "Z23", "Y3", "D1",
        "Q1", "Z14", "P1", "Z33", "D2", "Q2", "D3", "Q3", "Z24", "P2", "Z34", "P3", "C0", "C1", "C2", "C3",
    ):
        kind, at = token[0], int(token[1])
        if kind == "F":
            forward(at)
        elif kind == "S":
            second(at)
        elif kind == "X":
            along_x(at)
        elif kind == "Y":
            along_y(at)
        elif kind == "D":
            finish_x(at)
        elif kind == "P":
            hand_over(ends_z, at)
        elif kind == "Q":
            hand_over(ends_x, at)
        elif kind == "C":
            clear(at) if at < len(GROUPS) else clear_first()
        elif token[2] == "4":
            finish_z(at)
        else:
            advance(chains_z[at], unit_z(at), int(token[2]))

    def arrived(refs, sems):
        for place in range(8):
            pltpu.make_async_copy(refs.at[place], refs.at[place], sems.at[place]).wait()

    arrived(end_z, fin_z)
    total = end_z[0]
    for place in range(1, 8):
        total = total + end_z[place]
    first = jnp.concatenate([total[:, :64], total[:, 64:]], axis=0)
    arrived(end_x, fin_x)
    turn[...] = end_x[...].reshape(64, LANES).T
    second_half = turn[pl.ds(pl.multiple_of(core * ROWS, ROWS), ROWS), :]
    for p in range(2):
        lanes = slice(p * 32, p * 32 + 32)
        out_ref[p] = jnp.concatenate([first[:, lanes], second_half[:, lanes]], axis=1)

    for i in range(QUARTERS):
        wait_ends(ends_z[i])
        wait_ends(ends_x[i])


def body(green, green_bar):
    f32, bf16 = jnp.float32, jnp.bfloat16
    far = pl.BlockSpec(memory_space=pltpu.HBM)
    return pl.pallas_call(
        kernel,
        out_shape=jax.ShapeDtypeStruct((2, ROWS, ROWS), f32),
        in_specs=[far, far],
        out_specs=pl.BlockSpec(memory_space=pltpu.VMEM),
        scratch_shapes=[
            pltpu.VMEM((2, ROWS, N), f32),
            pltpu.VMEM((2, ROWS, N), f32),
            pltpu.VMEM((3, 2, ROWS, N), f32),
            pltpu.VMEM((3, 2, ROWS, N), f32),
            pltpu.VMEM((3, 2, ROWS, N), f32),
            pltpu.VMEM((512, 2 * N), bf16),
            pltpu.VMEM((512, 2 * N), bf16),
            pltpu.VMEM((256, 2 * N), bf16),
            pltpu.VMEM((256, 2 * N), bf16),
            pltpu.VMEM((512, 512), bf16),
            pltpu.VMEM((512, 512), bf16),
            pltpu.VMEM((512, N), bf16),
            pltpu.VMEM((512, N), bf16),
            pltpu.VMEM((Z, QUARTERS, 64, LANES), f32),
            pltpu.VMEM((X, QUARTERS, Z, 16, LANES), f32),
            pltpu.VMEM((HOPS, QUARTERS, 64, LANES), f32),
            pltpu.VMEM((HOPS, QUARTERS, 8, LANES), f32),
            pltpu.VMEM((3, QUARTERS, Z, 16, LANES), f32),
            pltpu.VMEM((2, QUARTERS, Z, 8, LANES), f32),
            pltpu.VMEM((QUARTERS, Z, 8, LANES), f32),
            pltpu.VMEM((Z, QUARTERS, 8, LANES), f32),
            pltpu.VMEM((QUARTERS, 2, 32, LANES), f32),
            pltpu.VMEM((QUARTERS, 8, LANES), f32),
            pltpu.VMEM((8, 32, LANES), f32),
            pltpu.VMEM((8, 8, LANES), f32),
            pltpu.VMEM((LANES, 64), f32),
            pltpu.SemaphoreType.DMA((COPIES,)),
            pltpu.SemaphoreType.DMA((COPIES,)),
            pltpu.SemaphoreType.DMA((8,)),
            pltpu.SemaphoreType.DMA((8,)),
            pltpu.SemaphoreType.DMA((2,)),
            pltpu.SemaphoreType.REGULAR((8,)),
        ],
        compiler_params=pltpu.CompilerParams(
            collective_id=0, has_side_effects=True, vmem_limit_bytes=63 * 1024 * 1024
        ),
        cost_estimate=pl.CostEstimate(flops=3 * 1073741824, bytes_accessed=1081344, transcendentals=0),
        name="dyson_adjoint",
    )(green, green_bar)


def solution(mesh):
    spec = P("freq", None, "orb", None)
    return jax.shard_map(
        body, mesh=mesh, in_specs=(spec, spec), out_specs=P(None, "orb", "freq"), check_vma=False
    )
```

```python
import jax
import jax.numpy as jnp
from jax import lax
from jax.experimental import pallas as pl
from jax.experimental.pallas import tpu as pltpu
from jax.sharding import PartitionSpec as P

ROWS = 64
N = 1024
QUARTERS = 4
GROUPS = ((0, 1), (1, 1), (2, 1), (3, 1))
WIDE = 256
LANES = 128
X, Z = 4, 8
HOPS = 7
COPIES = 160


def split(value):
    high = value.astype(jnp.bfloat16)
    return high, (value - high.astype(jnp.float32)).astype(jnp.bfloat16)


def matmul(left, right, transposed):
    dims = (((1,), (1 if transposed else 0,)), ((), ()))
    return lax.dot_general(left, right, dims, preferred_element_type=jnp.float32)


def three_pass(left_hi, left_lo, right_hi, right_lo, transposed):
    return (
        matmul(left_hi, right_hi, transposed)
        + matmul(left_hi, right_lo, transposed)
        + matmul(left_lo, right_hi, transposed)
    )


def device_at(x, h, z, low, core):
    return {"freq": z * 2 + low, "orb": x * 4 + h * 2 + core}


def kernel(
    g_hbm, b_hbm, out_ref,
    g, b, gc, ba, ga, l_hi, l_lo, w_hi, w_lo, m_hi, m_lo, a_hi, a_lo,
    part_z, part_x, got_z, got_x, sum_x, mid_x, sum_y, hop_x, own_z, own_x, end_z, end_x, turn,
    send, recv, fin_z, fin_x, load, nods,
):
    freq, orb = lax.axis_index("freq"), lax.axis_index("orb")
    z, low = freq // 2, freq % 2
    x, h, core = orb // 4, (orb // 2) % 2, orb % 2
    odd, pair = z % 2, z // 2

    x_next = device_at((x + 1) % X, h, z, low, core)
    x_far = device_at((x + 2) % X, h, z, low, core)
    x_prev = device_at((x + 3) % X, h, z, low, core)
    partner = device_at(x, 1 - h, z, low, core)
    other = device_at(x, h, z, low, 1 - core)
    z_next = device_at(x, h, (z + 1) % Z, low, core)
    z_prev = device_at(x, h, (z + 7) % Z, low, core)

    load_g = pltpu.make_async_copy(g_hbm.at[0], g, load.at[0])
    load_b = pltpu.make_async_copy(b_hbm.at[0], b, load.at[1])
    load_g.start()
    load_b.start()

    numbers = iter(range(COPIES))

    def copy(src, dst, target):
        number = next(numbers)
        return pltpu.make_async_remote_copy(
            src_ref=src, dst_ref=dst, send_sem=send.at[number], recv_sem=recv.at[number],
            device_id=target, device_id_type=pl.DeviceIdType.MESH,
        )

    barrier = pltpu.get_barrier_semaphore()

    def greet(target):
        pl.semaphore_signal(barrier, inc=1, device_id=target, device_id_type=pl.DeviceIdType.MESH)

    twin = device_at(x, h, z, 1 - low, core)
    for target in (x_next, x_prev, partner, other, z_next, z_prev, twin):
        greet(target)
    self_z = (h == odd) & (low == core)
    pl.semaphore_wait(barrier, 7)

    def nod(number, *targets):
        for target in targets:
            pl.semaphore_signal(
                nods.at[number], inc=1, device_id=target, device_id_type=pl.DeviceIdType.MESH
            )

    def wide(quarter):
        return pl.ds(quarter * WIDE, WIDE)

    def lanes_of(quarter, side):
        return pl.ds((quarter + 2 * side) % QUARTERS * WIDE + side * LANES, LANES)

    blocks = [[lanes_of(i, side) for side in range(2)] for i in range(QUARTERS)]

    gh, bh = g_hbm.at[0], b_hbm.at[0]
    yb = [copy(bh.at[p], ba.at[1, p], partner) for p in range(2)]
    xp = [copy(gh.at[p], gc.at[0, p], x_next) for p in range(2)]
    xm = [copy(gh.at[p], gc.at[1, p], x_prev) for p in range(2)]
    cb = copy(bh, ba.at[0], other)
    cg = copy(gh, ga.at[0], other)
    yg = [[copy(gh.at[:, :, k], ga.at[1, :, :, k], partner) for k in block] for block in blocks]
    for c in (yb[0], xp[0], xm[1], cb, yb[1], xp[1], xm[0], cg, *sum(yg, [])):
        c.start()
    xf = [copy(gc.at[0, 0], gc.at[2, 0], x_next), copy(gc.at[1, 1], gc.at[2, 1], x_prev)]
    cbf = [copy(ba.at[1, p], ba.at[2, p], other) for p in range(2)]
    cgf = [[copy(ga.at[1, :, :, k], ga.at[2, :, :, k], other) for k in block] for block in blocks]

    def fill_left(ref, place):
        high_r, low_r = split(ref[0])
        high_i, low_i = split(ref[1])
        for dst, re, im in ((l_hi, high_r, high_i), (l_lo, low_r, low_i)):
            for half in range(2):
                rows = slice(half * 32, half * 32 + 32)
                top = pl.ds(place * 128 + half * 64, 32)
                bottom = pl.ds(place * 128 + half * 64 + 32, 32)
                dst[top, :N] = re[rows]
                dst[top, N:] = -im[rows]
                dst[bottom, :N] = im[rows]
                dst[bottom, N:] = re[rows]

    def fill_bar(ref, slot):
        rows = pl.ds(slot * ROWS, ROWS)
        for p in range(2):
            w_hi[rows, pl.ds(p * N, N)], w_lo[rows, pl.ds(p * N, N)] = split(ref[p])

    def fill_rows(ref, slot, quarter):
        for p in range(2):
            rows = pl.ds(p * 256 + slot * ROWS, ROWS)
            for side in range(2):
                columns = pl.ds(quarter * WIDE + side * LANES, LANES)
                a_hi[rows, columns], a_lo[rows, columns] = split(ref[p, :, blocks[quarter][side]])

    def middle(start, count):
        rows = pl.ds(start * 128, count * 128)
        product = three_pass(l_hi[rows, :], l_lo[rows, :], w_hi[...], w_lo[...], True)
        for piece in range(start * 2, (start + count) * 2):
            at = (piece - start * 2) * 64
            re, im = product[at:at + 32], product[at + 32:at + 64]
            for first, second, rows in ((re, -im, pl.ds(piece * 64, 32)), (im, re, pl.ds(piece * 64 + 32, 32))):
                m_hi[rows, :256], m_lo[rows, :256] = split(first)
                m_hi[rows, 256:], m_lo[rows, 256:] = split(second)

    nod(0, z_next, z_prev)
    load_g.wait()
    fill_left(g, 0)
    for i in range(QUARTERS):
        fill_rows(g, 0, i)
    load_b.wait()
    fill_bar(b, 0)
    cb.wait_recv()
    fill_bar(ba.at[0], 1)
    cg.wait_recv()
    for i in range(QUARTERS):
        fill_rows(ga.at[0], 1, i)

    pl.semaphore_wait(nods.at[0], 2)
    nod(1, z_next, z_prev)
    nod(3, other)
    xp[0].wait_recv()
    xf[0].start()
    xm[1].wait_recv()
    xf[1].start()
    pl.semaphore_wait(nods.at[3], 1)
    nod(4, partner)
    yb[0].wait_recv()
    cbf[0].start()
    pl.semaphore_wait(nods.at[1], 2)
    nod(2, z_next, z_prev)
    pl.semaphore_wait(nods.at[4], 1)
    nod(5, twin)
    pl.semaphore_wait(nods.at[5], 1)
    nod(6, x_next, x_prev)
    xp[1].wait_recv()
    fill_left(gc.at[0], 2)
    xm[0].wait_recv()
    fill_left(gc.at[1], 1)
    pl.semaphore_wait(nods.at[2], 2)
    pl.semaphore_wait(nods.at[6], 2)
    nod(7, x_next, x_prev)
    yb[1].wait_recv()
    cbf[1].start()
    fill_bar(ba.at[1], 2)
    for c in cbf:
        c.wait_recv()
    fill_bar(ba.at[2], 3)
    pl.semaphore_wait(nods.at[7], 2)
    middle(0, 3)
    for side in range(2):
        yg[0][side].wait_recv()
        cgf[0][side].start()
    for c in xf:
        c.wait_recv()
    fill_left(gc.at[2], 3)
    middle(3, 1)

    def quarters(group):
        return pl.ds(*GROUPS[group])

    def chains_of(group, own_part, got):
        sign = 1 if group % 2 == 0 else -1
        at = quarters(group)
        chains = []
        for direction, hops, base in ((sign, 4, 0), (-sign, 3, 4)):
            target = z_next if direction == 1 else z_prev
            steps = []
            for s in range(hops):
                dest = (z + direction * (hops - s) + Z) % Z
                before = got.at[base + s - 1, at]
                steps.append((copy(own_part(dest) if s == 0 else before, got.at[base + s, at], target), dest, before))
            chains.append(steps)
        return chains

    def unit_z(group):
        return lambda dest: part_z.at[((dest // 2 - x + X) % X) * 2 + dest % 2, quarters(group)]

    def unit_x(group):
        return lambda dest: hop_x.at[dest, quarters(group)]

    chains_z = [chains_of(i, unit_z(i), got_z) for i in range(len(GROUPS))]
    direct_x = [
        [
            copy(unit_x(i)((z + o) % Z), got_x.at[o - 1, quarters(i)], device_at(x, h, (z + o) % Z, low, core))
            for o in (4, 3, 5, 2, 6, 1, 7)
        ]
        for i in range(len(GROUPS))
    ]
    to_twin = [copy(mid_x.at[1 - low, quarters(i)], sum_y.at[quarters(i)], twin) for i in range(len(GROUPS))]
    to_x = [
        [
            copy(part_x.at[(x + j) % X, quarters(i)], sum_x.at[j - 1, quarters(i)], target)
            for j, target in ((2, x_far), (1, x_next), (3, x_prev))
        ]
        for i in range(len(GROUPS))
    ]

    def advance(chains, own_part, s):
        for steps in chains:
            if s < len(steps):
                step, dest, before = steps[s]
                if s > 0:
                    steps[s - 1][0].wait_recv()
                    before[...] += own_part(dest)[...]
                step.start()

    def end_copy(src, dst, arrived, target, itself):
        number = next(numbers)
        remote = pltpu.make_async_remote_copy(
            src_ref=src, dst_ref=dst, send_sem=send.at[number], recv_sem=arrived,
            device_id=target, device_id_type=pl.DeviceIdType.MESH,
        )
        return remote, pltpu.make_async_copy(src, dst, arrived), itself

    place_z = place_x = x * 2 + low
    ends_z = [[
        end_copy(
            own_z.at[i, half], end_z.at[place_z], fin_z.at[place_z],
            device_at((i + 2 * odd) % X, odd, 2 * pair + h, core, half),
            self_z & (x == (i + 2 * odd) % X) & (core == half),
        ) for half in range(2)] for i in range(QUARTERS)]
    ends_x = [[
        end_copy(
            own_x.at[i], end_x.at[place_x], fin_x.at[place_x],
            device_at((i + 2 * odd) % X, odd, 2 * pair + h, core, half),
            self_z & (x == (i + 2 * odd) % X) & (core == half),
        ) for half in range(2)] for i in range(QUARTERS)]

    def start_ends(ends):
        for remote, local, itself in ends:
            @pl.when(itself)
            def _():
                local.start()

            @pl.when(jnp.logical_not(itself))
            def _():
                remote.start()

    def wait_ends(ends):
        for remote, local, itself in ends:
            @pl.when(jnp.logical_not(itself))
            def _():
                remote.wait_send()

    def forward(quarter):
        for side in range(2):
            yg[quarter][side].wait_recv()
            cgf[quarter][side].start()

    def second(group):
        start, count = GROUPS[group]
        for quarter in range(start, start + count):
            cols = wide(quarter)
            fill_rows(ga.at[1], 2, quarter)
            for c in cgf[quarter]:
                c.wait_recv()
            fill_rows(ga.at[2], 3, quarter)
            total = three_pass(m_hi[...], m_lo[...], a_hi[:, cols], a_lo[:, cols], False)
            for place, j in ((0, 0), (1, 1), (2, 3), (3, 2)):
                for side in range(2):
                    lanes = slice(side * LANES, (side + 1) * LANES)
                    part_z[j * 2 + side, quarter] = total[place * 128:place * 128 + 64, lanes]
                    for k in range(X):
                        rows = place * 128 + 64 + k * 16
                        part_x[k, quarter, 2 * ((x + j) % X) + side] = total[rows:rows + 16, lanes]
        for c in to_x[group]:
            c.start()
        advance(chains_z[group], unit_z(group), 0)

    def along_x(group):
        for c in to_x[group]:
            c.wait_recv()
        start, count = GROUPS[group]
        for i in range(start, start + count):
            total = (part_x[x, i] + sum_x[0, i]) + (sum_x[1, i] + sum_x[2, i])
            for part in range(2):
                mid_x[part, i] = total[:, part * 8:part * 8 + 8]
        to_twin[group].start()

    def along_y(group):
        to_twin[group].wait_recv()
        start, count = GROUPS[group]
        for i in range(start, start + count):
            hop_x[:, i] = mid_x[low, i] + sum_y[i]
        for c in direct_x[group]:
            c.start()

    def finish_z(group):
        for steps in chains_z[group]:
            steps[-1][0].wait_recv()
        start, count = GROUPS[group]
        sums = unit_z(group)(z)[...] + got_z[3, quarters(group)] + got_z[6, quarters(group)]
        for i in range(count):
            flipped = sums[i].T
            for half in range(2):
                top = flipped[half * 64:half * 64 + 32]
                bottom = flipped[half * 64 + 32:half * 64 + 64]
                own_z[start + i, half] = jnp.concatenate([top, bottom], axis=1)

    def finish_x(group):
        start, count = GROUPS[group]
        at = quarters(group)
        for c in direct_x[group]:
            c.wait_recv()
        sums = hop_x[z, at] + got_x[0, at]
        for o in range(1, 7):
            sums = sums + got_x[o, at]
        own_x[at] = sums

    def hand_over(ends, group):
        start, count = GROUPS[group]
        for i in range(start, start + count):
            start_ends(ends[i])

    def clear_first():
        for c in (*xp, *xm, *xf, cb, cg, *yb, *cbf):
            c.wait_send()

    def clear(group):
        for c in to_x[group]:
            c.wait_send()
        start, count = GROUPS[group]
        for i in range(start, start + count):
            for c in (*yg[i], *cgf[i]):
                c.wait_send()
        for steps in chains_z[group]:
            for step, _, _ in steps:
                step.wait_send()
        to_twin[group].wait_send()
        for c in direct_x[group]:
            c.wait_send()

    for token in (
        "F1", "S0", "F2", "S1", "F3", "Z01", "S2", "Z11", "X0", "S3", "Z02", "Z21", "X1", "Z12", "Z31", "Y0",
        "X2", "Z03", "Z22", "C9", "Y1", "X3", "Z13", "Z32", "Y2", "Z04", "P0", "D0", "Q0", "Z23", "Y3",
        "Z14", "P1", "D1", "Q1", "Z33", "Z24", "P2", "D2", "Q2", "Z34", "P3", "D3", "Q3", "C0", "C1", "C2",
        "C3",
    ):
        kind, at = token[0], int(token[1])
        if kind == "F":
            forward(at)
        elif kind == "S":
            second(at)
        elif kind == "X":
            along_x(at)
        elif kind == "Y":
            along_y(at)
        elif kind == "D":
            finish_x(at)
        elif kind == "P":
            hand_over(ends_z, at)
        elif kind == "Q":
            hand_over(ends_x, at)
        elif kind == "C":
            clear(at) if at < len(GROUPS) else clear_first()
        elif token[2] == "4":
            finish_z(at)
        else:
            advance(chains_z[at], unit_z(at), int(token[2]))

    def arrived(refs, sems):
        for place in range(8):
            pltpu.make_async_copy(refs.at[place], refs.at[place], sems.at[place]).wait()

    arrived(end_z, fin_z)
    total = end_z[0]
    for place in range(1, 8):
        total = total + end_z[place]
    first = jnp.concatenate([total[:, :64], total[:, 64:]], axis=0)
    arrived(end_x, fin_x)
    turn[...] = end_x[...].reshape(64, LANES).T
    second_half = turn[pl.ds(pl.multiple_of(core * ROWS, ROWS), ROWS), :]
    for p in range(2):
        lanes = slice(p * 32, p * 32 + 32)
        out_ref[p] = jnp.concatenate([first[:, lanes], second_half[:, lanes]], axis=1)

    for i in range(QUARTERS):
        wait_ends(ends_z[i])
        wait_ends(ends_x[i])


def body(green, green_bar):
    f32, bf16 = jnp.float32, jnp.bfloat16
    far = pl.BlockSpec(memory_space=pltpu.HBM)
    return pl.pallas_call(
        kernel,
        out_shape=jax.ShapeDtypeStruct((2, ROWS, ROWS), f32),
        in_specs=[far, far],
        out_specs=pl.BlockSpec(memory_space=pltpu.VMEM),
        scratch_shapes=[
            pltpu.VMEM((2, ROWS, N), f32),
            pltpu.VMEM((2, ROWS, N), f32),
            pltpu.VMEM((3, 2, ROWS, N), f32),
            pltpu.VMEM((3, 2, ROWS, N), f32),
            pltpu.VMEM((3, 2, ROWS, N), f32),
            pltpu.VMEM((512, 2 * N), bf16),
            pltpu.VMEM((512, 2 * N), bf16),
            pltpu.VMEM((256, 2 * N), bf16),
            pltpu.VMEM((256, 2 * N), bf16),
            pltpu.VMEM((512, 512), bf16),
            pltpu.VMEM((512, 512), bf16),
            pltpu.VMEM((512, N), bf16),
            pltpu.VMEM((512, N), bf16),
            pltpu.VMEM((Z, QUARTERS, 64, LANES), f32),
            pltpu.VMEM((X, QUARTERS, Z, 16, LANES), f32),
            pltpu.VMEM((HOPS, QUARTERS, 64, LANES), f32),
            pltpu.VMEM((HOPS, QUARTERS, 8, LANES), f32),
            pltpu.VMEM((3, QUARTERS, Z, 16, LANES), f32),
            pltpu.VMEM((2, QUARTERS, Z, 8, LANES), f32),
            pltpu.VMEM((QUARTERS, Z, 8, LANES), f32),
            pltpu.VMEM((Z, QUARTERS, 8, LANES), f32),
            pltpu.VMEM((QUARTERS, 2, 32, LANES), f32),
            pltpu.VMEM((QUARTERS, 8, LANES), f32),
            pltpu.VMEM((8, 32, LANES), f32),
            pltpu.VMEM((8, 8, LANES), f32),
            pltpu.VMEM((LANES, 64), f32),
            pltpu.SemaphoreType.DMA((COPIES,)),
            pltpu.SemaphoreType.DMA((COPIES,)),
            pltpu.SemaphoreType.DMA((8,)),
            pltpu.SemaphoreType.DMA((8,)),
            pltpu.SemaphoreType.DMA((2,)),
            pltpu.SemaphoreType.REGULAR((8,)),
        ],
        compiler_params=pltpu.CompilerParams(
            collective_id=0, has_side_effects=True, vmem_limit_bytes=54912 * 1024
        ),
        cost_estimate=pl.CostEstimate(flops=3 * 1073741824, bytes_accessed=1081344, transcendentals=0),
        name="dyson_adjoint",
    )(green, green_bar)


def solution(mesh):
    spec = P("freq", None, "orb", None)
    return jax.shard_map(
        body, mesh=mesh, in_specs=(spec, spec), out_specs=P(None, "orb", "freq"), check_vma=False
    )
```

```python
import jax
import jax.numpy as jnp
from jax import lax
from jax.experimental import pallas as pl
from jax.experimental.pallas import tpu as pltpu
from jax.sharding import PartitionSpec as P

ROWS = 64
N = 1024
QUARTERS = 4
GROUPS = ((0, 1), (1, 1), (2, 1), (3, 1))
WIDE = 256
LANES = 128
X, Z = 4, 8
HOPS = 7
COPIES = 160


def split(value):
    high = value.astype(jnp.bfloat16)
    return high, (value - high.astype(jnp.float32)).astype(jnp.bfloat16)


def matmul(left, right, transposed):
    dims = (((1,), (1 if transposed else 0,)), ((), ()))
    return lax.dot_general(left, right, dims, preferred_element_type=jnp.float32)


def three_pass(left_hi, left_lo, right_hi, right_lo, transposed):
    return (
        matmul(left_hi, right_hi, transposed)
        + matmul(left_hi, right_lo, transposed)
        + matmul(left_lo, right_hi, transposed)
    )


def device_at(x, h, z, low, core):
    return {"freq": z * 2 + low, "orb": x * 4 + h * 2 + core}


def kernel(
    g_hbm, b_hbm, out_ref,
    g, b, gc, ba, ga, l_hi, l_lo, w_hi, w_lo, m_hi, m_lo, a_hi, a_lo,
    part_z, part_x, got_z, got_x, sum_x, mid_x, sum_y, hop_x, own_z, own_x, end_z, end_x, turn,
    send, recv, fin_z, fin_x, load, nods,
):
    freq, orb = lax.axis_index("freq"), lax.axis_index("orb")
    z, low = freq // 2, freq % 2
    x, h, core = orb // 4, (orb // 2) % 2, orb % 2
    odd, pair = z % 2, z // 2

    x_next = device_at((x + 1) % X, h, z, low, core)
    x_far = device_at((x + 2) % X, h, z, low, core)
    x_prev = device_at((x + 3) % X, h, z, low, core)
    partner = device_at(x, 1 - h, z, low, core)
    other = device_at(x, h, z, low, 1 - core)
    z_next = device_at(x, h, (z + 1) % Z, low, core)
    z_prev = device_at(x, h, (z + 7) % Z, low, core)

    load_g = pltpu.make_async_copy(g_hbm.at[0], g, load.at[0])
    load_b = pltpu.make_async_copy(b_hbm.at[0], b, load.at[1])
    load_g.start()
    load_b.start()

    numbers = iter(range(COPIES))

    def copy(src, dst, target):
        number = next(numbers)
        return pltpu.make_async_remote_copy(
            src_ref=src, dst_ref=dst, send_sem=send.at[number], recv_sem=recv.at[number],
            device_id=target, device_id_type=pl.DeviceIdType.MESH,
        )

    barrier = pltpu.get_barrier_semaphore()

    def greet(target):
        pl.semaphore_signal(barrier, inc=1, device_id=target, device_id_type=pl.DeviceIdType.MESH)

    twin = device_at(x, h, z, 1 - low, core)
    for target in (x_next, x_prev, partner, other, z_next, z_prev, twin):
        greet(target)
    self_z = (h == odd) & (low == core)
    pl.semaphore_wait(barrier, 7)

    def nod(number, *targets):
        for target in targets:
            pl.semaphore_signal(
                nods.at[number], inc=1, device_id=target, device_id_type=pl.DeviceIdType.MESH
            )

    def wide(quarter):
        return pl.ds(quarter * WIDE, WIDE)

    def lanes_of(quarter, side):
        return pl.ds((quarter + 2 * side) % QUARTERS * WIDE + side * LANES, LANES)

    blocks = [[lanes_of(i, side) for side in range(2)] for i in range(QUARTERS)]

    gh, bh = g_hbm.at[0], b_hbm.at[0]
    yb = [copy(bh.at[p], ba.at[1, p], partner) for p in range(2)]
    xp = [copy(gh.at[p], gc.at[0, p], x_next) for p in range(2)]
    xm = [copy(gh.at[p], gc.at[1, p], x_prev) for p in range(2)]
    cb = copy(bh, ba.at[0], other)
    cg = copy(gh, ga.at[0], other)
    yg = [[copy(gh.at[:, :, k], ga.at[1, :, :, k], partner) for k in block] for block in blocks]
    for c in (yb[0], xp[0], xm[1], cb, yb[1], xp[1], xm[0], cg, *sum(yg, [])):
        c.start()
    xf = [copy(gc.at[0, 0], gc.at[2, 0], x_next), copy(gc.at[1, 1], gc.at[2, 1], x_prev)]
    cbf = [copy(ba.at[1, p], ba.at[2, p], other) for p in range(2)]
    cgf = [[copy(ga.at[1, :, :, k], ga.at[2, :, :, k], other) for k in block] for block in blocks]

    def fill_left(ref, place):
        high_r, low_r = split(ref[0])
        high_i, low_i = split(ref[1])
        for dst, re, im in ((l_hi, high_r, high_i), (l_lo, low_r, low_i)):
            for half in range(2):
                rows = slice(half * 32, half * 32 + 32)
                top = pl.ds(place * 128 + half * 64, 32)
                bottom = pl.ds(place * 128 + half * 64 + 32, 32)
                dst[top, :N] = re[rows]
                dst[top, N:] = -im[rows]
                dst[bottom, :N] = im[rows]
                dst[bottom, N:] = re[rows]

    def fill_bar(ref, slot):
        rows = pl.ds(slot * ROWS, ROWS)
        for p in range(2):
            w_hi[rows, pl.ds(p * N, N)], w_lo[rows, pl.ds(p * N, N)] = split(ref[p])

    def fill_rows(ref, slot, quarter):
        for p in range(2):
            rows = pl.ds(p * 256 + slot * ROWS, ROWS)
            for side in range(2):
                columns = pl.ds(quarter * WIDE + side * LANES, LANES)
                a_hi[rows, columns], a_lo[rows, columns] = split(ref[p, :, blocks[quarter][side]])

    def middle(start, count):
        rows = pl.ds(start * 128, count * 128)
        product = three_pass(l_hi[rows, :], l_lo[rows, :], w_hi[...], w_lo[...], True)
        for piece in range(start * 2, (start + count) * 2):
            at = (piece - start * 2) * 64
            re, im = product[at:at + 32], product[at + 32:at + 64]
            for first, second, rows in ((re, -im, pl.ds(piece * 64, 32)), (im, re, pl.ds(piece * 64 + 32, 32))):
                m_hi[rows, :256], m_lo[rows, :256] = split(first)
                m_hi[rows, 256:], m_lo[rows, 256:] = split(second)

    nod(0, z_next, z_prev)
    load_g.wait()
    fill_left(g, 0)
    for i in range(QUARTERS):
        fill_rows(g, 0, i)
    load_b.wait()
    fill_bar(b, 0)
    cb.wait_recv()
    fill_bar(ba.at[0], 1)
    cg.wait_recv()
    for i in range(QUARTERS):
        fill_rows(ga.at[0], 1, i)

    pl.semaphore_wait(nods.at[0], 2)
    nod(1, z_next, z_prev)
    nod(3, other)
    xp[0].wait_recv()
    xf[0].start()
    xm[1].wait_recv()
    xf[1].start()
    pl.semaphore_wait(nods.at[3], 1)
    nod(4, partner)
    yb[0].wait_recv()
    cbf[0].start()
    pl.semaphore_wait(nods.at[1], 2)
    nod(2, z_next, z_prev)
    pl.semaphore_wait(nods.at[4], 1)
    nod(5, twin)
    pl.semaphore_wait(nods.at[5], 1)
    nod(6, x_next, x_prev)
    xp[1].wait_recv()
    fill_left(gc.at[0], 2)
    xm[0].wait_recv()
    fill_left(gc.at[1], 1)
    pl.semaphore_wait(nods.at[2], 2)
    pl.semaphore_wait(nods.at[6], 2)
    nod(7, x_next, x_prev)
    yb[1].wait_recv()
    cbf[1].start()
    fill_bar(ba.at[1], 2)
    for c in cbf:
        c.wait_recv()
    fill_bar(ba.at[2], 3)
    pl.semaphore_wait(nods.at[7], 2)
    middle(0, 3)
    for side in range(2):
        yg[0][side].wait_recv()
        cgf[0][side].start()
    for c in xf:
        c.wait_recv()
    fill_left(gc.at[2], 3)
    middle(3, 1)

    def quarters(group):
        return pl.ds(*GROUPS[group])

    def chains_of(group, own_part, got):
        sign = 1 if group % 2 == 0 else -1
        at = quarters(group)
        chains = []
        for direction, hops, base in ((sign, 4, 0), (-sign, 3, 4)):
            target = z_next if direction == 1 else z_prev
            steps = []
            for s in range(hops):
                dest = (z + direction * (hops - s) + Z) % Z
                before = got.at[base + s - 1, at]
                steps.append((copy(own_part(dest) if s == 0 else before, got.at[base + s, at], target), dest, before))
            chains.append(steps)
        return chains

    def unit_z(group):
        return lambda dest: part_z.at[((dest // 2 - x + X) % X) * 2 + dest % 2, quarters(group)]

    def unit_x(group):
        return lambda dest: hop_x.at[dest, quarters(group)]

    chains_z = [chains_of(i, unit_z(i), got_z) for i in range(len(GROUPS))]
    direct_x = [
        [
            copy(unit_x(i)((z + o) % Z), got_x.at[o - 1, quarters(i)], device_at(x, h, (z + o) % Z, low, core))
            for o in (4, 3, 5, 2, 6, 1, 7)
        ]
        for i in range(len(GROUPS))
    ]
    to_twin = [copy(mid_x.at[1 - low, quarters(i)], sum_y.at[quarters(i)], twin) for i in range(len(GROUPS))]
    to_x = [
        [
            copy(part_x.at[(x + j) % X, quarters(i)], sum_x.at[j - 1, quarters(i)], target)
            for j, target in ((2, x_far), (1, x_next), (3, x_prev))
        ]
        for i in range(len(GROUPS))
    ]

    def advance(chains, own_part, s):
        for steps in chains:
            if s < len(steps):
                step, dest, before = steps[s]
                if s > 0:
                    steps[s - 1][0].wait_recv()
                    before[...] += own_part(dest)[...]
                step.start()

    def end_copy(src, dst, arrived, target, itself):
        number = next(numbers)
        remote = pltpu.make_async_remote_copy(
            src_ref=src, dst_ref=dst, send_sem=send.at[number], recv_sem=arrived,
            device_id=target, device_id_type=pl.DeviceIdType.MESH,
        )
        return remote, pltpu.make_async_copy(src, dst, arrived), itself

    place_z = place_x = x * 2 + low
    ends_z = [[
        end_copy(
            own_z.at[i, half], end_z.at[place_z], fin_z.at[place_z],
            device_at((i + 2 * odd) % X, odd, 2 * pair + h, core, half),
            self_z & (x == (i + 2 * odd) % X) & (core == half),
        ) for half in range(2)] for i in range(QUARTERS)]
    ends_x = [[
        end_copy(
            own_x.at[i], end_x.at[place_x], fin_x.at[place_x],
            device_at((i + 2 * odd) % X, odd, 2 * pair + h, core, half),
            self_z & (x == (i + 2 * odd) % X) & (core == half),
        ) for half in range(2)] for i in range(QUARTERS)]

    def start_ends(ends):
        for remote, local, itself in ends:
            @pl.when(itself)
            def _():
                local.start()

            @pl.when(jnp.logical_not(itself))
            def _():
                remote.start()

    def wait_ends(ends):
        for remote, local, itself in ends:
            @pl.when(jnp.logical_not(itself))
            def _():
                remote.wait_send()

    def forward(quarter):
        for side in range(2):
            yg[quarter][side].wait_recv()
            cgf[quarter][side].start()

    def second(group):
        start, count = GROUPS[group]
        for quarter in range(start, start + count):
            cols = wide(quarter)
            fill_rows(ga.at[1], 2, quarter)
            for c in cgf[quarter]:
                c.wait_recv()
            fill_rows(ga.at[2], 3, quarter)
            total = three_pass(m_hi[...], m_lo[...], a_hi[:, cols], a_lo[:, cols], False)
            for place, j in ((0, 0), (1, 1), (2, 3), (3, 2)):
                for side in range(2):
                    lanes = slice(side * LANES, (side + 1) * LANES)
                    part_z[j * 2 + side, quarter] = total[place * 128:place * 128 + 64, lanes]
                    for k in range(X):
                        rows = place * 128 + 64 + k * 16
                        part_x[k, quarter, 2 * ((x + j) % X) + side] = total[rows:rows + 16, lanes]
        for c in to_x[group]:
            c.start()
        advance(chains_z[group], unit_z(group), 0)

    def along_x(group):
        for c in to_x[group]:
            c.wait_recv()
        start, count = GROUPS[group]
        for i in range(start, start + count):
            total = (part_x[x, i] + sum_x[0, i]) + (sum_x[1, i] + sum_x[2, i])
            for part in range(2):
                mid_x[part, i] = total[:, part * 8:part * 8 + 8]
        to_twin[group].start()

    def along_y(group):
        to_twin[group].wait_recv()
        start, count = GROUPS[group]
        for i in range(start, start + count):
            hop_x[:, i] = mid_x[low, i] + sum_y[i]
        for c in direct_x[group]:
            c.start()

    def finish_z(group):
        for steps in chains_z[group]:
            steps[-1][0].wait_recv()
        start, count = GROUPS[group]
        sums = unit_z(group)(z)[...] + got_z[3, quarters(group)] + got_z[6, quarters(group)]
        for i in range(count):
            flipped = sums[i].T
            for half in range(2):
                top = flipped[half * 64:half * 64 + 32]
                bottom = flipped[half * 64 + 32:half * 64 + 64]
                own_z[start + i, half] = jnp.concatenate([top, bottom], axis=1)

    def finish_x(group):
        start, count = GROUPS[group]
        at = quarters(group)
        for c in direct_x[group]:
            c.wait_recv()
        sums = hop_x[z, at] + got_x[0, at]
        for o in range(1, 7):
            sums = sums + got_x[o, at]
        own_x[at] = sums

    def hand_over(ends, group):
        start, count = GROUPS[group]
        for i in range(start, start + count):
            start_ends(ends[i])

    def clear_first():
        for c in (*xp, *xm, *xf, cb, cg, *yb, *cbf):
            c.wait_send()

    def clear(group):
        for c in to_x[group]:
            c.wait_send()
        start, count = GROUPS[group]
        for i in range(start, start + count):
            for c in (*yg[i], *cgf[i]):
                c.wait_send()
        for steps in chains_z[group]:
            for step, _, _ in steps:
                step.wait_send()
        to_twin[group].wait_send()
        for c in direct_x[group]:
            c.wait_send()

    for token in (
        "F1", "S0", "F2", "S1", "F3", "Z01", "S2", "Z11", "X0", "S3", "Z02", "Z21", "X1", "Z12", "Z31", "Y0",
        "X2", "Z03", "Z22", "C9", "Y1", "X3", "Z13", "Z32", "Y2", "Z04", "D0", "Z23", "Y3", "Z14", "P0",
        "Q0", "Z33", "D1", "P1", "Q1", "Z24", "D2", "Z34", "P2", "Q2", "P3", "D3", "Q3", "C0", "C1", "C2",
        "C3",
    ):
        kind, at = token[0], int(token[1])
        if kind == "F":
            forward(at)
        elif kind == "S":
            second(at)
        elif kind == "X":
            along_x(at)
        elif kind == "Y":
            along_y(at)
        elif kind == "D":
            finish_x(at)
        elif kind == "P":
            hand_over(ends_z, at)
        elif kind == "Q":
            hand_over(ends_x, at)
        elif kind == "C":
            clear(at) if at < len(GROUPS) else clear_first()
        elif token[2] == "4":
            finish_z(at)
        else:
            advance(chains_z[at], unit_z(at), int(token[2]))

    def arrived(refs, sems):
        for place in range(8):
            pltpu.make_async_copy(refs.at[place], refs.at[place], sems.at[place]).wait()

    for i in range(QUARTERS - 1):
        wait_ends(ends_z[i])
        wait_ends(ends_x[i])
    arrived(end_z, fin_z)
    total = end_z[0]
    for place in range(1, 8):
        total = total + end_z[place]
    first = jnp.concatenate([total[:, :64], total[:, 64:]], axis=0)
    arrived(end_x, fin_x)
    turn[...] = end_x[...].reshape(64, LANES).T
    second_half = turn[pl.ds(pl.multiple_of(core * ROWS, ROWS), ROWS), :]
    for p in range(2):
        lanes = slice(p * 32, p * 32 + 32)
        out_ref[p] = jnp.concatenate([first[:, lanes], second_half[:, lanes]], axis=1)

    for i in range(QUARTERS - 1, QUARTERS):
        wait_ends(ends_z[i])
        wait_ends(ends_x[i])


def body(green, green_bar):
    f32, bf16 = jnp.float32, jnp.bfloat16
    far = pl.BlockSpec(memory_space=pltpu.HBM)
    return pl.pallas_call(
        kernel,
        out_shape=jax.ShapeDtypeStruct((2, ROWS, ROWS), f32),
        in_specs=[far, far],
        out_specs=pl.BlockSpec(memory_space=pltpu.VMEM),
        scratch_shapes=[
            pltpu.VMEM((2, ROWS, N), f32),
            pltpu.VMEM((2, ROWS, N), f32),
            pltpu.VMEM((3, 2, ROWS, N), f32),
            pltpu.VMEM((3, 2, ROWS, N), f32),
            pltpu.VMEM((3, 2, ROWS, N), f32),
            pltpu.VMEM((512, 2 * N), bf16),
            pltpu.VMEM((512, 2 * N), bf16),
            pltpu.VMEM((256, 2 * N), bf16),
            pltpu.VMEM((256, 2 * N), bf16),
            pltpu.VMEM((512, 512), bf16),
            pltpu.VMEM((512, 512), bf16),
            pltpu.VMEM((512, N), bf16),
            pltpu.VMEM((512, N), bf16),
            pltpu.VMEM((Z, QUARTERS, 64, LANES), f32),
            pltpu.VMEM((X, QUARTERS, Z, 16, LANES), f32),
            pltpu.VMEM((HOPS, QUARTERS, 64, LANES), f32),
            pltpu.VMEM((HOPS, QUARTERS, 8, LANES), f32),
            pltpu.VMEM((3, QUARTERS, Z, 16, LANES), f32),
            pltpu.VMEM((2, QUARTERS, Z, 8, LANES), f32),
            pltpu.VMEM((QUARTERS, Z, 8, LANES), f32),
            pltpu.VMEM((Z, QUARTERS, 8, LANES), f32),
            pltpu.VMEM((QUARTERS, 2, 32, LANES), f32),
            pltpu.VMEM((QUARTERS, 8, LANES), f32),
            pltpu.VMEM((8, 32, LANES), f32),
            pltpu.VMEM((8, 8, LANES), f32),
            pltpu.VMEM((LANES, 64), f32),
            pltpu.SemaphoreType.DMA((COPIES,)),
            pltpu.SemaphoreType.DMA((COPIES,)),
            pltpu.SemaphoreType.DMA((8,)),
            pltpu.SemaphoreType.DMA((8,)),
            pltpu.SemaphoreType.DMA((2,)),
            pltpu.SemaphoreType.REGULAR((8,)),
        ],
        compiler_params=pltpu.CompilerParams(
            collective_id=0, has_side_effects=True, vmem_limit_bytes=54912 * 1024
        ),
        cost_estimate=pl.CostEstimate(flops=3 * 1073741824, bytes_accessed=1081344, transcendentals=0),
        name="dyson_adjoint",
    )(green, green_bar)


def solution(mesh):
    spec = P("freq", None, "orb", None)
    return jax.shard_map(
        body, mesh=mesh, in_specs=(spec, spec), out_specs=P(None, "orb", "freq"), check_vma=False
    )
```

```python
import jax
import jax.numpy as jnp
from jax import lax
from jax.experimental import pallas as pl
from jax.experimental.pallas import tpu as pltpu
from jax.sharding import PartitionSpec as P

ROWS = 64
N = 1024
QUARTERS = 4
GROUPS = ((0, 1), (1, 1), (2, 1), (3, 1))
WIDE = 256
LANES = 128
X, Z = 4, 8
HOPS = 7
COPIES = 160


def split(value):
    high = value.astype(jnp.bfloat16)
    return high, (value - high.astype(jnp.float32)).astype(jnp.bfloat16)


def matmul(left, right, transposed):
    dims = (((1,), (1 if transposed else 0,)), ((), ()))
    return lax.dot_general(left, right, dims, preferred_element_type=jnp.float32)


def three_pass(left_hi, left_lo, right_hi, right_lo, transposed):
    return (
        matmul(left_hi, right_hi, transposed)
        + matmul(left_hi, right_lo, transposed)
        + matmul(left_lo, right_hi, transposed)
    )


def device_at(x, h, z, low, core):
    return {"freq": z * 2 + low, "orb": x * 4 + h * 2 + core}


def kernel(
    g_hbm, b_hbm, out_ref,
    g, b, gc, ba, ga, l_hi, l_lo, w_hi, w_lo, m_hi, m_lo, a_hi, a_lo,
    part_z, part_x, got_z, got_x, sum_x, mid_x, sum_y, hop_x, own_z, own_x, end_z, end_x, turn,
    send, recv, fin_z, fin_x, load, nods,
):
    freq, orb = lax.axis_index("freq"), lax.axis_index("orb")
    z, low = freq // 2, freq % 2
    x, h, core = orb // 4, (orb // 2) % 2, orb % 2
    odd, pair = z % 2, z // 2

    x_next = device_at((x + 1) % X, h, z, low, core)
    x_far = device_at((x + 2) % X, h, z, low, core)
    x_prev = device_at((x + 3) % X, h, z, low, core)
    partner = device_at(x, 1 - h, z, low, core)
    other = device_at(x, h, z, low, 1 - core)
    z_next = device_at(x, h, (z + 1) % Z, low, core)
    z_prev = device_at(x, h, (z + 7) % Z, low, core)

    load_g = pltpu.make_async_copy(g_hbm.at[0], g, load.at[0])
    load_b = pltpu.make_async_copy(b_hbm.at[0], b, load.at[1])
    load_g.start()
    load_b.start()

    numbers = iter(range(COPIES))

    def copy(src, dst, target):
        number = next(numbers)
        return pltpu.make_async_remote_copy(
            src_ref=src, dst_ref=dst, send_sem=send.at[number], recv_sem=recv.at[number],
            device_id=target, device_id_type=pl.DeviceIdType.MESH,
        )

    barrier = pltpu.get_barrier_semaphore()

    def greet(target):
        pl.semaphore_signal(barrier, inc=1, device_id=target, device_id_type=pl.DeviceIdType.MESH)

    twin = device_at(x, h, z, 1 - low, core)
    for target in (x_next, x_prev, partner, other, z_next, z_prev, twin):
        greet(target)
    self_z = (h == odd) & (low == core)
    pl.semaphore_wait(barrier, 7)

    def nod(number, *targets):
        for target in targets:
            pl.semaphore_signal(
                nods.at[number], inc=1, device_id=target, device_id_type=pl.DeviceIdType.MESH
            )

    def wide(quarter):
        return pl.ds(quarter * WIDE, WIDE)

    def lanes_of(quarter, side):
        return pl.ds((quarter + 2 * side) % QUARTERS * WIDE + side * LANES, LANES)

    blocks = [[lanes_of(i, side) for side in range(2)] for i in range(QUARTERS)]

    gh, bh = g_hbm.at[0], b_hbm.at[0]
    yb = [copy(bh.at[p], ba.at[1, p], partner) for p in range(2)]
    xp = [copy(gh.at[p], gc.at[0, p], x_next) for p in range(2)]
    xm = [copy(gh.at[p], gc.at[1, p], x_prev) for p in range(2)]
    cb = copy(bh, ba.at[0], other)
    cg = copy(gh, ga.at[0], other)
    yg = [[copy(gh.at[:, :, k], ga.at[1, :, :, k], partner) for k in block] for block in blocks]
    for c in (yb[0], xp[0], xm[1], cb, yb[1], xp[1], xm[0], cg, *sum(yg, [])):
        c.start()
    xf = [copy(gc.at[0, 0], gc.at[2, 0], x_next), copy(gc.at[1, 1], gc.at[2, 1], x_prev)]
    cbf = [copy(ba.at[1, p], ba.at[2, p], other) for p in range(2)]
    cgf = [[copy(ga.at[1, :, :, k], ga.at[2, :, :, k], other) for k in block] for block in blocks]

    def fill_left(ref, place):
        high_r, low_r = split(ref[0])
        high_i, low_i = split(ref[1])
        for dst, re, im in ((l_hi, high_r, high_i), (l_lo, low_r, low_i)):
            for half in range(2):
                rows = slice(half * 32, half * 32 + 32)
                top = pl.ds(place * 128 + half * 64, 32)
                bottom = pl.ds(place * 128 + half * 64 + 32, 32)
                dst[top, :N] = re[rows]
                dst[top, N:] = -im[rows]
                dst[bottom, :N] = im[rows]
                dst[bottom, N:] = re[rows]

    def fill_bar(ref, slot):
        rows = pl.ds(slot * ROWS, ROWS)
        for p in range(2):
            w_hi[rows, pl.ds(p * N, N)], w_lo[rows, pl.ds(p * N, N)] = split(ref[p])

    def fill_rows(ref, slot, quarter):
        for p in range(2):
            rows = pl.ds(p * 256 + slot * ROWS, ROWS)
            for side in range(2):
                columns = pl.ds(quarter * WIDE + side * LANES, LANES)
                a_hi[rows, columns], a_lo[rows, columns] = split(ref[p, :, blocks[quarter][side]])

    def middle(start, count):
        rows = pl.ds(start * 128, count * 128)
        product = three_pass(l_hi[rows, :], l_lo[rows, :], w_hi[...], w_lo[...], True)
        for piece in range(start * 2, (start + count) * 2):
            at = (piece - start * 2) * 64
            re, im = product[at:at + 32], product[at + 32:at + 64]
            for first, second, rows in ((re, -im, pl.ds(piece * 64, 32)), (im, re, pl.ds(piece * 64 + 32, 32))):
                m_hi[rows, :256], m_lo[rows, :256] = split(first)
                m_hi[rows, 256:], m_lo[rows, 256:] = split(second)

    nod(0, z_next, z_prev)
    load_g.wait()
    fill_left(g, 0)
    for i in range(QUARTERS):
        fill_rows(g, 0, i)
    load_b.wait()
    fill_bar(b, 0)
    cb.wait_recv()
    fill_bar(ba.at[0], 1)
    cg.wait_recv()
    for i in range(QUARTERS):
        fill_rows(ga.at[0], 1, i)

    pl.semaphore_wait(nods.at[0], 2)
    nod(1, z_next, z_prev)
    nod(3, other)
    xp[0].wait_recv()
    xf[0].start()
    xm[1].wait_recv()
    xf[1].start()
    pl.semaphore_wait(nods.at[3], 1)
    nod(4, partner)
    yb[0].wait_recv()
    cbf[0].start()
    pl.semaphore_wait(nods.at[1], 2)
    nod(2, z_next, z_prev)
    pl.semaphore_wait(nods.at[4], 1)
    nod(5, twin)
    pl.semaphore_wait(nods.at[5], 1)
    nod(6, x_next, x_prev)
    xp[1].wait_recv()
    fill_left(gc.at[0], 2)
    xm[0].wait_recv()
    fill_left(gc.at[1], 1)
    pl.semaphore_wait(nods.at[2], 2)
    pl.semaphore_wait(nods.at[6], 2)
    nod(7, x_next, x_prev)
    yb[1].wait_recv()
    cbf[1].start()
    fill_bar(ba.at[1], 2)
    for c in cbf:
        c.wait_recv()
    fill_bar(ba.at[2], 3)
    pl.semaphore_wait(nods.at[7], 2)
    middle(0, 3)
    for side in range(2):
        yg[0][side].wait_recv()
        cgf[0][side].start()
    for c in xf:
        c.wait_recv()
    fill_left(gc.at[2], 3)
    middle(3, 1)

    def quarters(group):
        return pl.ds(*GROUPS[group])

    def chains_of(group, own_part, got):
        sign = 1 if group % 2 == 0 else -1
        at = quarters(group)
        chains = []
        for direction, hops, base in ((sign, 4, 0), (-sign, 3, 4)):
            target = z_next if direction == 1 else z_prev
            steps = []
            for s in range(hops):
                dest = (z + direction * (hops - s) + Z) % Z
                before = got.at[base + s - 1, at]
                steps.append((copy(own_part(dest) if s == 0 else before, got.at[base + s, at], target), dest, before))
            chains.append(steps)
        return chains

    def unit_z(group):
        return lambda dest: part_z.at[((dest // 2 - x + X) % X) * 2 + dest % 2, quarters(group)]

    def unit_x(group):
        return lambda dest: hop_x.at[dest, quarters(group)]

    chains_z = [chains_of(i, unit_z(i), got_z) for i in range(len(GROUPS))]
    direct_x = [
        [
            copy(unit_x(i)((z + o) % Z), got_x.at[o - 1, quarters(i)], device_at(x, h, (z + o) % Z, low, core))
            for o in (4, 3, 5, 2, 6, 1, 7)
        ]
        for i in range(len(GROUPS))
    ]
    to_twin = [copy(mid_x.at[1 - low, quarters(i)], sum_y.at[quarters(i)], twin) for i in range(len(GROUPS))]
    to_x = [
        [
            copy(part_x.at[(x + j) % X, quarters(i)], sum_x.at[j - 1, quarters(i)], target)
            for j, target in ((2, x_far), (1, x_next), (3, x_prev))
        ]
        for i in range(len(GROUPS))
    ]

    def advance(chains, own_part, s):
        for steps in chains:
            if s < len(steps):
                step, dest, before = steps[s]
                if s > 0:
                    steps[s - 1][0].wait_recv()
                    before[...] += own_part(dest)[...]
                step.start()

    def end_copy(src, dst, arrived, target, itself):
        number = next(numbers)
        remote = pltpu.make_async_remote_copy(
            src_ref=src, dst_ref=dst, send_sem=send.at[number], recv_sem=arrived,
            device_id=target, device_id_type=pl.DeviceIdType.MESH,
        )
        return remote, pltpu.make_async_copy(src, dst, arrived), itself

    place_z = place_x = x * 2 + low
    ends_z = [[
        end_copy(
            own_z.at[i, half], end_z.at[place_z], fin_z.at[place_z],
            device_at((i + 2 * odd) % X, odd, 2 * pair + h, core, half),
            self_z & (x == (i + 2 * odd) % X) & (core == half),
        ) for half in range(2)] for i in range(QUARTERS)]
    ends_x = [[
        end_copy(
            own_x.at[i], end_x.at[place_x], fin_x.at[place_x],
            device_at((i + 2 * odd) % X, odd, 2 * pair + h, core, half),
            self_z & (x == (i + 2 * odd) % X) & (core == half),
        ) for half in range(2)] for i in range(QUARTERS)]

    def start_ends(ends):
        for remote, local, itself in ends:
            @pl.when(itself)
            def _():
                local.start()

            @pl.when(jnp.logical_not(itself))
            def _():
                remote.start()

    def wait_ends(ends):
        for remote, local, itself in ends:
            @pl.when(jnp.logical_not(itself))
            def _():
                remote.wait_send()

    def forward(quarter):
        for side in range(2):
            yg[quarter][side].wait_recv()
            cgf[quarter][side].start()

    def second(group):
        start, count = GROUPS[group]
        for quarter in range(start, start + count):
            cols = wide(quarter)
            fill_rows(ga.at[1], 2, quarter)
            for c in cgf[quarter]:
                c.wait_recv()
            fill_rows(ga.at[2], 3, quarter)
            total = three_pass(m_hi[...], m_lo[...], a_hi[:, cols], a_lo[:, cols], False)
            for place, j in ((0, 0), (1, 1), (2, 3), (3, 2)):
                for side in range(2):
                    lanes = slice(side * LANES, (side + 1) * LANES)
                    part_z[j * 2 + side, quarter] = total[place * 128:place * 128 + 64, lanes]
                    for k in range(X):
                        rows = place * 128 + 64 + k * 16
                        part_x[k, quarter, 2 * ((x + j) % X) + side] = total[rows:rows + 16, lanes]
        advance(chains_z[group], unit_z(group), 0)
        for c in to_x[group]:
            c.start()

    def along_x(group):
        for c in to_x[group]:
            c.wait_recv()
        start, count = GROUPS[group]
        for i in range(start, start + count):
            total = (part_x[x, i] + sum_x[0, i]) + (sum_x[1, i] + sum_x[2, i])
            for part in range(2):
                mid_x[part, i] = total[:, part * 8:part * 8 + 8]
        to_twin[group].start()

    def along_y(group):
        to_twin[group].wait_recv()
        start, count = GROUPS[group]
        for i in range(start, start + count):
            hop_x[:, i] = mid_x[low, i] + sum_y[i]
        for c in direct_x[group]:
            c.start()

    def finish_z(group):
        for steps in chains_z[group]:
            steps[-1][0].wait_recv()
        start, count = GROUPS[group]
        sums = unit_z(group)(z)[...] + got_z[3, quarters(group)] + got_z[6, quarters(group)]
        for i in range(count):
            flipped = sums[i].T
            for half in range(2):
                top = flipped[half * 64:half * 64 + 32]
                bottom = flipped[half * 64 + 32:half * 64 + 64]
                own_z[start + i, half] = jnp.concatenate([top, bottom], axis=1)

    def finish_x(group):
        start, count = GROUPS[group]
        at = quarters(group)
        for c in direct_x[group]:
            c.wait_recv()
        sums = hop_x[z, at] + got_x[0, at]
        for o in range(1, 7):
            sums = sums + got_x[o, at]
        own_x[at] = sums

    def hand_over(ends, group):
        start, count = GROUPS[group]
        for i in range(start, start + count):
            start_ends(ends[i])

    def clear_first():
        for c in (*xp, *xm, *xf, cb, cg, *yb, *cbf):
            c.wait_send()

    def clear(group):
        for c in to_x[group]:
            c.wait_send()
        start, count = GROUPS[group]
        for i in range(start, start + count):
            for c in (*yg[i], *cgf[i]):
                c.wait_send()
        for steps in chains_z[group]:
            for step, _, _ in steps:
                step.wait_send()
        to_twin[group].wait_send()
        for c in direct_x[group]:
            c.wait_send()

    for token in (
        "F1", "S0", "F2", "S1", "F3", "Z01", "S2", "Z11", "X0", "S3", "Z02", "Z21", "X1", "Z12", "Z31", "Y0",
        "X2", "Z03", "Z22", "C9", "Y1", "X3", "Z13", "Z32", "Y2", "Z04", "D0", "Z23", "Y3", "Z14", "P0",
        "Q0", "Z33", "D1", "P1", "Q1", "Z24", "D2", "Z34", "P2", "Q2", "P3", "D3", "Q3", "C0", "C1", "C2",
        "C3",
    ):
        kind, at = token[0], int(token[1])
        if kind == "F":
            forward(at)
        elif kind == "S":
            second(at)
        elif kind == "X":
            along_x(at)
        elif kind == "Y":
            along_y(at)
        elif kind == "D":
            finish_x(at)
        elif kind == "P":
            hand_over(ends_z, at)
        elif kind == "Q":
            hand_over(ends_x, at)
        elif kind == "C":
            clear(at) if at < len(GROUPS) else clear_first()
        elif token[2] == "4":
            finish_z(at)
        else:
            advance(chains_z[at], unit_z(at), int(token[2]))

    def arrived(refs, sems, place):
        pltpu.make_async_copy(refs.at[place], refs.at[place], sems.at[place]).wait()

    for i in range(QUARTERS - 1):
        wait_ends(ends_z[i])
        wait_ends(ends_x[i])
    arrived(end_z, fin_z, 0)
    total = end_z[0]
    for place in range(1, 8):
        arrived(end_z, fin_z, place)
        total = total + end_z[place]
    first = jnp.concatenate([total[:, :64], total[:, 64:]], axis=0)
    for place in range(8):
        arrived(end_x, fin_x, place)
    turn[...] = end_x[...].reshape(64, LANES).T
    second_half = turn[pl.ds(pl.multiple_of(core * ROWS, ROWS), ROWS), :]
    for p in range(2):
        lanes = slice(p * 32, p * 32 + 32)
        out_ref[p] = jnp.concatenate([first[:, lanes], second_half[:, lanes]], axis=1)

    for i in range(QUARTERS - 1, QUARTERS):
        wait_ends(ends_z[i])
        wait_ends(ends_x[i])


def body(green, green_bar):
    f32, bf16 = jnp.float32, jnp.bfloat16
    far = pl.BlockSpec(memory_space=pltpu.HBM)
    return pl.pallas_call(
        kernel,
        out_shape=jax.ShapeDtypeStruct((2, ROWS, ROWS), f32),
        in_specs=[far, far],
        out_specs=pl.BlockSpec(memory_space=pltpu.VMEM),
        scratch_shapes=[
            pltpu.VMEM((2, ROWS, N), f32),
            pltpu.VMEM((2, ROWS, N), f32),
            pltpu.VMEM((3, 2, ROWS, N), f32),
            pltpu.VMEM((3, 2, ROWS, N), f32),
            pltpu.VMEM((3, 2, ROWS, N), f32),
            pltpu.VMEM((512, 2 * N), bf16),
            pltpu.VMEM((512, 2 * N), bf16),
            pltpu.VMEM((256, 2 * N), bf16),
            pltpu.VMEM((256, 2 * N), bf16),
            pltpu.VMEM((512, 512), bf16),
            pltpu.VMEM((512, 512), bf16),
            pltpu.VMEM((512, N), bf16),
            pltpu.VMEM((512, N), bf16),
            pltpu.VMEM((Z, QUARTERS, 64, LANES), f32),
            pltpu.VMEM((X, QUARTERS, Z, 16, LANES), f32),
            pltpu.VMEM((HOPS, QUARTERS, 64, LANES), f32),
            pltpu.VMEM((HOPS, QUARTERS, 8, LANES), f32),
            pltpu.VMEM((3, QUARTERS, Z, 16, LANES), f32),
            pltpu.VMEM((2, QUARTERS, Z, 8, LANES), f32),
            pltpu.VMEM((QUARTERS, Z, 8, LANES), f32),
            pltpu.VMEM((Z, QUARTERS, 8, LANES), f32),
            pltpu.VMEM((QUARTERS, 2, 32, LANES), f32),
            pltpu.VMEM((QUARTERS, 8, LANES), f32),
            pltpu.VMEM((8, 32, LANES), f32),
            pltpu.VMEM((8, 8, LANES), f32),
            pltpu.VMEM((LANES, 64), f32),
            pltpu.SemaphoreType.DMA((COPIES,)),
            pltpu.SemaphoreType.DMA((COPIES,)),
            pltpu.SemaphoreType.DMA((8,)),
            pltpu.SemaphoreType.DMA((8,)),
            pltpu.SemaphoreType.DMA((2,)),
            pltpu.SemaphoreType.REGULAR((8,)),
        ],
        compiler_params=pltpu.CompilerParams(
            collective_id=0, has_side_effects=True, vmem_limit_bytes=54912 * 1024
        ),
        cost_estimate=pl.CostEstimate(flops=3 * 1073741824, bytes_accessed=1081344, transcendentals=0),
        name="dyson_adjoint",
    )(green, green_bar)


def solution(mesh):
    spec = P("freq", None, "orb", None)
    return jax.shard_map(
        body, mesh=mesh, in_specs=(spec, spec), out_specs=P(None, "orb", "freq"), check_vma=False
    )
```

```python
import jax
import jax.numpy as jnp
from jax import lax
from jax.experimental import pallas as pl
from jax.experimental.pallas import tpu as pltpu
from jax.sharding import PartitionSpec as P

ROWS = 64
N = 1024
QUARTERS = 4
GROUPS = ((0, 1), (1, 1), (2, 1), (3, 1))
WIDE = 256
LANES = 128
X, Z = 4, 8
HOPS = 7
COPIES = 160


def split(value):
    high = value.astype(jnp.bfloat16)
    return high, (value - high.astype(jnp.float32)).astype(jnp.bfloat16)


def matmul(left, right, transposed):
    dims = (((1,), (1 if transposed else 0,)), ((), ()))
    return lax.dot_general(left, right, dims, preferred_element_type=jnp.float32)


def three_pass(left_hi, left_lo, right_hi, right_lo, transposed):
    return (
        matmul(left_hi, right_hi, transposed)
        + matmul(left_hi, right_lo, transposed)
        + matmul(left_lo, right_hi, transposed)
    )


def device_at(x, h, z, low, core):
    return {"freq": z * 2 + low, "orb": x * 4 + h * 2 + core}


def kernel(
    g_hbm, b_hbm, out_ref,
    g, b, gc, ba, ga, l_hi, l_lo, w_hi, w_lo, m_hi, m_lo, a_hi, a_lo,
    part_z, part_x, got_z, got_x, sum_x, mid_x, sum_y, hop_x, own_z, own_x, end_z, end_x, turn,
    send, recv, fin_z, fin_x, load, nods,
):
    freq, orb = lax.axis_index("freq"), lax.axis_index("orb")
    z, low = freq // 2, freq % 2
    x, h, core = orb // 4, (orb // 2) % 2, orb % 2
    odd, pair = z % 2, z // 2

    x_next = device_at((x + 1) % X, h, z, low, core)
    x_far = device_at((x + 2) % X, h, z, low, core)
    x_prev = device_at((x + 3) % X, h, z, low, core)
    partner = device_at(x, 1 - h, z, low, core)
    other = device_at(x, h, z, low, 1 - core)
    z_next = device_at(x, h, (z + 1) % Z, low, core)
    z_prev = device_at(x, h, (z + 7) % Z, low, core)

    load_g = pltpu.make_async_copy(g_hbm.at[0], g, load.at[0])
    load_b = pltpu.make_async_copy(b_hbm.at[0], b, load.at[1])
    load_g.start()
    load_b.start()

    numbers = iter(range(COPIES))

    def copy(src, dst, target):
        number = next(numbers)
        return pltpu.make_async_remote_copy(
            src_ref=src, dst_ref=dst, send_sem=send.at[number], recv_sem=recv.at[number],
            device_id=target, device_id_type=pl.DeviceIdType.MESH,
        )

    barrier = pltpu.get_barrier_semaphore()

    def greet(target):
        pl.semaphore_signal(barrier, inc=1, device_id=target, device_id_type=pl.DeviceIdType.MESH)

    twin = device_at(x, h, z, 1 - low, core)
    for target in (x_next, x_prev, partner, other, z_next, z_prev, twin):
        greet(target)
    self_z = (h == odd) & (low == core)
    pl.semaphore_wait(barrier, 7)

    def nod(number, *targets):
        for target in targets:
            pl.semaphore_signal(
                nods.at[number], inc=1, device_id=target, device_id_type=pl.DeviceIdType.MESH
            )

    def wide(quarter):
        return pl.ds(quarter * WIDE, WIDE)

    def lanes_of(quarter, side):
        return pl.ds((quarter + 2 * side) % QUARTERS * WIDE + side * LANES, LANES)

    blocks = [[lanes_of(i, side) for side in range(2)] for i in range(QUARTERS)]

    gh, bh = g_hbm.at[0], b_hbm.at[0]
    yb = [copy(bh.at[p], ba.at[1, p], partner) for p in range(2)]
    xp = [copy(gh.at[p], gc.at[0, p], x_next) for p in range(2)]
    xm = [copy(gh.at[p], gc.at[1, p], x_prev) for p in range(2)]
    cb = copy(bh, ba.at[0], other)
    cg = copy(gh, ga.at[0], other)
    yg = [[copy(gh.at[:, :, k], ga.at[1, :, :, k], partner) for k in block] for block in blocks]
    for c in (xp[0], xm[1], yb[0], cb, xp[1], xm[0], yb[1], cg, *sum(yg, [])):
        c.start()
    xf = [copy(gc.at[0, 0], gc.at[2, 0], x_next), copy(gc.at[1, 1], gc.at[2, 1], x_prev)]
    cbf = [copy(ba.at[1, p], ba.at[2, p], other) for p in range(2)]
    cgf = [[copy(ga.at[1, :, :, k], ga.at[2, :, :, k], other) for k in block] for block in blocks]

    def fill_left(ref, place):
        high_r, low_r = split(ref[0])
        high_i, low_i = split(ref[1])
        for dst, re, im in ((l_hi, high_r, high_i), (l_lo, low_r, low_i)):
            for half in range(2):
                rows = slice(half * 32, half * 32 + 32)
                top = pl.ds(place * 128 + half * 64, 32)
                bottom = pl.ds(place * 128 + half * 64 + 32, 32)
                dst[top, :N] = re[rows]
                dst[top, N:] = -im[rows]
                dst[bottom, :N] = im[rows]
                dst[bottom, N:] = re[rows]

    def fill_bar(ref, slot):
        rows = pl.ds(slot * ROWS, ROWS)
        for p in range(2):
            w_hi[rows, pl.ds(p * N, N)], w_lo[rows, pl.ds(p * N, N)] = split(ref[p])

    def fill_rows(ref, slot, quarter):
        for p in range(2):
            rows = pl.ds(p * 256 + slot * ROWS, ROWS)
            for side in range(2):
                columns = pl.ds(quarter * WIDE + side * LANES, LANES)
                a_hi[rows, columns], a_lo[rows, columns] = split(ref[p, :, blocks[quarter][side]])

    def middle(start, count):
        rows = pl.ds(start * 128, count * 128)
        product = three_pass(l_hi[rows, :], l_lo[rows, :], w_hi[...], w_lo[...], True)
        for piece in range(start * 2, (start + count) * 2):
            at = (piece - start * 2) * 64
            re, im = product[at:at + 32], product[at + 32:at + 64]
            for first, second, rows in ((re, -im, pl.ds(piece * 64, 32)), (im, re, pl.ds(piece * 64 + 32, 32))):
                m_hi[rows, :256], m_lo[rows, :256] = split(first)
                m_hi[rows, 256:], m_lo[rows, 256:] = split(second)

    nod(0, z_next, z_prev)
    load_g.wait()
    fill_left(g, 0)
    for i in range(QUARTERS):
        fill_rows(g, 0, i)
    load_b.wait()
    fill_bar(b, 0)
    cb.wait_recv()
    fill_bar(ba.at[0], 1)
    cg.wait_recv()
    for i in range(QUARTERS):
        fill_rows(ga.at[0], 1, i)

    pl.semaphore_wait(nods.at[0], 2)
    nod(1, z_next, z_prev)
    nod(3, other)
    xp[0].wait_recv()
    xf[0].start()
    xm[1].wait_recv()
    xf[1].start()
    pl.semaphore_wait(nods.at[3], 1)
    nod(4, partner)
    yb[0].wait_recv()
    cbf[0].start()
    pl.semaphore_wait(nods.at[1], 2)
    nod(2, z_next, z_prev)
    pl.semaphore_wait(nods.at[4], 1)
    nod(5, twin)
    pl.semaphore_wait(nods.at[5], 1)
    nod(6, x_next, x_prev)
    xp[1].wait_recv()
    fill_left(gc.at[0], 2)
    xm[0].wait_recv()
    fill_left(gc.at[1], 1)
    pl.semaphore_wait(nods.at[2], 2)
    pl.semaphore_wait(nods.at[6], 2)
    nod(7, x_next, x_prev)
    yb[1].wait_recv()
    cbf[1].start()
    fill_bar(ba.at[1], 2)
    for c in cbf:
        c.wait_recv()
    fill_bar(ba.at[2], 3)
    pl.semaphore_wait(nods.at[7], 2)
    middle(0, 3)
    for side in range(2):
        yg[0][side].wait_recv()
        cgf[0][side].start()
    for c in xf:
        c.wait_recv()
    fill_left(gc.at[2], 3)
    middle(3, 1)

    def quarters(group):
        return pl.ds(*GROUPS[group])

    def chains_of(group, own_part, got):
        sign = 1 if group % 2 == 0 else -1
        at = quarters(group)
        chains = []
        for direction, hops, base in ((sign, 4, 0), (-sign, 3, 4)):
            target = z_next if direction == 1 else z_prev
            steps = []
            for s in range(hops):
                dest = (z + direction * (hops - s) + Z) % Z
                before = got.at[base + s - 1, at]
                steps.append((copy(own_part(dest) if s == 0 else before, got.at[base + s, at], target), dest, before))
            chains.append(steps)
        return chains

    def unit_z(group):
        return lambda dest: part_z.at[((dest // 2 - x + X) % X) * 2 + dest % 2, quarters(group)]

    def unit_x(group):
        return lambda dest: hop_x.at[dest, quarters(group)]

    chains_z = [chains_of(i, unit_z(i), got_z) for i in range(len(GROUPS))]
    direct_x = [
        [
            copy(unit_x(i)((z + o) % Z), got_x.at[o - 1, quarters(i)], device_at(x, h, (z + o) % Z, low, core))
            for o in (4, 3, 5, 2, 6, 1, 7)
        ]
        for i in range(len(GROUPS))
    ]
    to_twin = [copy(mid_x.at[1 - low, quarters(i)], sum_y.at[quarters(i)], twin) for i in range(len(GROUPS))]
    to_x = [
        [
            copy(part_x.at[(x + j) % X, quarters(i)], sum_x.at[j - 1, quarters(i)], target)
            for j, target in ((2, x_far), (1, x_next), (3, x_prev))
        ]
        for i in range(len(GROUPS))
    ]

    def advance(chains, own_part, s):
        for steps in chains:
            if s < len(steps):
                step, dest, before = steps[s]
                if s > 0:
                    steps[s - 1][0].wait_recv()
                    before[...] += own_part(dest)[...]
                step.start()

    def end_copy(src, dst, arrived, target, itself):
        number = next(numbers)
        remote = pltpu.make_async_remote_copy(
            src_ref=src, dst_ref=dst, send_sem=send.at[number], recv_sem=arrived,
            device_id=target, device_id_type=pl.DeviceIdType.MESH,
        )
        return remote, pltpu.make_async_copy(src, dst, arrived), itself

    place_z = place_x = x * 2 + low
    ends_z = [[
        end_copy(
            own_z.at[i, half], end_z.at[place_z], fin_z.at[place_z],
            device_at((i + 2 * odd) % X, odd, 2 * pair + h, core, half),
            self_z & (x == (i + 2 * odd) % X) & (core == half),
        ) for half in range(2)] for i in range(QUARTERS)]
    ends_x = [[
        end_copy(
            own_x.at[i], end_x.at[place_x], fin_x.at[place_x],
            device_at((i + 2 * odd) % X, odd, 2 * pair + h, core, half),
            self_z & (x == (i + 2 * odd) % X) & (core == half),
        ) for half in range(2)] for i in range(QUARTERS)]

    def start_ends(ends):
        for remote, local, itself in ends:
            @pl.when(itself)
            def _():
                local.start()

            @pl.when(jnp.logical_not(itself))
            def _():
                remote.start()

    def wait_ends(ends):
        for remote, local, itself in ends:
            @pl.when(jnp.logical_not(itself))
            def _():
                remote.wait_send()

    def forward(quarter):
        for side in range(2):
            yg[quarter][side].wait_recv()
            cgf[quarter][side].start()

    def second(group):
        start, count = GROUPS[group]
        for quarter in range(start, start + count):
            cols = wide(quarter)
            fill_rows(ga.at[1], 2, quarter)
            for c in cgf[quarter]:
                c.wait_recv()
            fill_rows(ga.at[2], 3, quarter)
            total = three_pass(m_hi[...], m_lo[...], a_hi[:, cols], a_lo[:, cols], False)
            for place, j in ((0, 0), (1, 1), (2, 3), (3, 2)):
                for side in range(2):
                    lanes = slice(side * LANES, (side + 1) * LANES)
                    part_z[j * 2 + side, quarter] = total[place * 128:place * 128 + 64, lanes]
                    for k in range(X):
                        rows = place * 128 + 64 + k * 16
                        part_x[k, quarter, 2 * ((x + j) % X) + side] = total[rows:rows + 16, lanes]
        advance(chains_z[group], unit_z(group), 0)
        for c in to_x[group]:
            c.start()

    def along_x(group):
        for c in to_x[group]:
            c.wait_recv()
        start, count = GROUPS[group]
        for i in range(start, start + count):
            total = (part_x[x, i] + sum_x[0, i]) + (sum_x[1, i] + sum_x[2, i])
            for part in range(2):
                mid_x[part, i] = total[:, part * 8:part * 8 + 8]
        to_twin[group].start()

    def along_y(group):
        to_twin[group].wait_recv()
        start, count = GROUPS[group]
        for i in range(start, start + count):
            hop_x[:, i] = mid_x[low, i] + sum_y[i]
        for c in direct_x[group]:
            c.start()

    def finish_z(group):
        for steps in chains_z[group]:
            steps[-1][0].wait_recv()
        start, count = GROUPS[group]
        sums = unit_z(group)(z)[...] + got_z[3, quarters(group)] + got_z[6, quarters(group)]
        for i in range(count):
            flipped = sums[i].T
            for half in range(2):
                top = flipped[half * 64:half * 64 + 32]
                bottom = flipped[half * 64 + 32:half * 64 + 64]
                own_z[start + i, half] = jnp.concatenate([top, bottom], axis=1)

    def finish_x(group):
        start, count = GROUPS[group]
        at = quarters(group)
        for c in direct_x[group]:
            c.wait_recv()
        sums = hop_x[z, at] + got_x[0, at]
        for o in range(1, 7):
            sums = sums + got_x[o, at]
        own_x[at] = sums

    def hand_over(ends, group):
        start, count = GROUPS[group]
        for i in range(start, start + count):
            start_ends(ends[i])

    def clear_first():
        for c in (*xp, *xm, *xf, cb, cg, *yb, *cbf):
            c.wait_send()

    def clear(group):
        for c in to_x[group]:
            c.wait_send()
        start, count = GROUPS[group]
        for i in range(start, start + count):
            for c in (*yg[i], *cgf[i]):
                c.wait_send()
        for steps in chains_z[group]:
            for step, _, _ in steps:
                step.wait_send()
        to_twin[group].wait_send()
        for c in direct_x[group]:
            c.wait_send()

    for token in (
        "F1", "S0", "F2", "S1", "F3", "Z01", "S2", "Z11", "X0", "S3", "Z02", "Z21", "X1", "Z12", "Z31", "Y0",
        "X2", "Z03", "Z22", "C9", "Y1", "X3", "Z13", "Z32", "Y2", "Z04", "D0", "Z23", "Y3", "Z14", "P0",
        "Q0", "Z33", "D1", "P1", "Q1", "Z24", "D2", "Z34", "P2", "Q2", "P3", "D3", "Q3", "C0", "C1", "C2",
        "C3",
    ):
        kind, at = token[0], int(token[1])
        if kind == "F":
            forward(at)
        elif kind == "S":
            second(at)
        elif kind == "X":
            along_x(at)
        elif kind == "Y":
            along_y(at)
        elif kind == "D":
            finish_x(at)
        elif kind == "P":
            hand_over(ends_z, at)
        elif kind == "Q":
            hand_over(ends_x, at)
        elif kind == "C":
            clear(at) if at < len(GROUPS) else clear_first()
        elif token[2] == "4":
            finish_z(at)
        else:
            advance(chains_z[at], unit_z(at), int(token[2]))

    def arrived(refs, sems, place):
        pltpu.make_async_copy(refs.at[place], refs.at[place], sems.at[place]).wait()

    for i in range(QUARTERS - 1):
        wait_ends(ends_z[i])
        wait_ends(ends_x[i])
    arrived(end_z, fin_z, 0)
    total = end_z[0]
    for place in range(1, 8):
        arrived(end_z, fin_z, place)
        total = total + end_z[place]
    first = jnp.concatenate([total[:, :64], total[:, 64:]], axis=0)
    for place in range(8):
        arrived(end_x, fin_x, place)
    turn[...] = end_x[...].reshape(64, LANES).T
    second_half = turn[pl.ds(pl.multiple_of(core * ROWS, ROWS), ROWS), :]
    for p in range(2):
        lanes = slice(p * 32, p * 32 + 32)
        out_ref[p] = jnp.concatenate([first[:, lanes], second_half[:, lanes]], axis=1)

    for i in range(QUARTERS - 1, QUARTERS):
        wait_ends(ends_z[i])
        wait_ends(ends_x[i])


def body(green, green_bar):
    f32, bf16 = jnp.float32, jnp.bfloat16
    far = pl.BlockSpec(memory_space=pltpu.HBM)
    return pl.pallas_call(
        kernel,
        out_shape=jax.ShapeDtypeStruct((2, ROWS, ROWS), f32),
        in_specs=[far, far],
        out_specs=pl.BlockSpec(memory_space=pltpu.VMEM),
        scratch_shapes=[
            pltpu.VMEM((2, ROWS, N), f32),
            pltpu.VMEM((2, ROWS, N), f32),
            pltpu.VMEM((3, 2, ROWS, N), f32),
            pltpu.VMEM((3, 2, ROWS, N), f32),
            pltpu.VMEM((3, 2, ROWS, N), f32),
            pltpu.VMEM((512, 2 * N), bf16),
            pltpu.VMEM((512, 2 * N), bf16),
            pltpu.VMEM((256, 2 * N), bf16),
            pltpu.VMEM((256, 2 * N), bf16),
            pltpu.VMEM((512, 512), bf16),
            pltpu.VMEM((512, 512), bf16),
            pltpu.VMEM((512, N), bf16),
            pltpu.VMEM((512, N), bf16),
            pltpu.VMEM((Z, QUARTERS, 64, LANES), f32),
            pltpu.VMEM((X, QUARTERS, Z, 16, LANES), f32),
            pltpu.VMEM((HOPS, QUARTERS, 64, LANES), f32),
            pltpu.VMEM((HOPS, QUARTERS, 8, LANES), f32),
            pltpu.VMEM((3, QUARTERS, Z, 16, LANES), f32),
            pltpu.VMEM((2, QUARTERS, Z, 8, LANES), f32),
            pltpu.VMEM((QUARTERS, Z, 8, LANES), f32),
            pltpu.VMEM((Z, QUARTERS, 8, LANES), f32),
            pltpu.VMEM((QUARTERS, 2, 32, LANES), f32),
            pltpu.VMEM((QUARTERS, 8, LANES), f32),
            pltpu.VMEM((8, 32, LANES), f32),
            pltpu.VMEM((8, 8, LANES), f32),
            pltpu.VMEM((LANES, 64), f32),
            pltpu.SemaphoreType.DMA((COPIES,)),
            pltpu.SemaphoreType.DMA((COPIES,)),
            pltpu.SemaphoreType.DMA((8,)),
            pltpu.SemaphoreType.DMA((8,)),
            pltpu.SemaphoreType.DMA((2,)),
            pltpu.SemaphoreType.REGULAR((8,)),
        ],
        compiler_params=pltpu.CompilerParams(
            collective_id=0, has_side_effects=True, vmem_limit_bytes=54912 * 1024
        ),
        cost_estimate=pl.CostEstimate(flops=3 * 1073741824, bytes_accessed=1081344, transcendentals=0),
        name="dyson_adjoint",
    )(green, green_bar)


def solution(mesh):
    spec = P("freq", None, "orb", None)
    return jax.shard_map(
        body, mesh=mesh, in_specs=(spec, spec), out_specs=P(None, "orb", "freq"), check_vma=False
    )
```
